256 devices in a mesh: group: 32 (over y, z), seq: 8 (over x, core).
Axes of the slice: x: 4, y: 4, z: 8, core: 2. Of those that a mesh axis runs over, the one named last changes fastest.
Arguments:
- embed_table: bfloat16 [8192, 1024], P('group'), may hold values from -6 to 6
- adam_m: float32 [8192, 1024], P('group'), may hold values from -0.6 to 0.6
- adam_v: float32 [8192, 1024], P('group'), may hold values from 0.003 to 0.03
- lengths: int32 [32, 4], P('group'), may hold values from 1 to 1024, 2048 in all within a row
- row_owner: int32 [65536, 1], P(('group', 'seq')), may hold values from 0 to 31; in each aligned block of 256 rows (0 to 255, 256 to 511, ...) at most 16 rows name the same one
- row_index: int32 [65536], P(('group', 'seq')), may hold values from 0 to 255
- proj_weight: bfloat16 [1024, 4096], P(None, 'seq'), may hold values from -0.1875 to 0.1875
- out_weight: bfloat16 [1024, 1024], replicated, may hold values from -0.1875 to 0.1875
- norm_gain: float32 [1024], replicated, may hold values from 0.1 to 1.9
- upstream: bfloat16 [65536, 1024], P(('group', 'seq')), may hold values from -6 to 6
Outputs:
- layer_out: float32 [65536, 1024], P(('group', 'seq'))
- new_table: float32 [8192, 1024], P('group')
- new_moment: float32 [8192, 1024], P('group')
- new_second: float32 [8192, 1024], P('group')
The draws below stay inside these ranges and needn't reach their ends.
Inputs may be any that keep to these rules, and one draw needn't show every extreme that they name: `row_owner`: among the 256 tokens of one device (aligned blocks), no owner is named more than 16 times, a bound that some block reaches. Each group's lengths sum to 2048; the longest is exactly 2048 // 2.
All inputs are finite; a program needn't handle non-finite values.
Results may differ from the reference program's by a relative error of at most 0.0053.
Values may be sent and summed in bfloat16 or wider, within the bound.
A program may use at most 128 MiB of HBM per device.

```python
import math
import jax
import jax.numpy as jnp
import numpy as np
from jax import lax

D = 1024
HEADS = 16
DH = 64
HIST = 4
TOK_DEV = 256
TROWS = 256
VDIM = 1024
GROUP_TOK = 2048
TOTAL_TOK = 65536
CAP = 16
ROWS_ALL = 8192
N_GROUP = 32
N_SEQ = 8


def set_ends(values, stream_key, low, top_value):
    index_at = [jax.random.randint(jax.random.fold_in(stream_key, axis), (), 0, length) for axis, length in enumerate(values.shape)]
    main_axis = values.shape.index(max(values.shape))
    next_to = index_at[:main_axis] + [(index_at[main_axis] + 1) % values.shape[main_axis]] + index_at[main_axis + 1:]
    return values.at[tuple(index_at)].set(low).at[tuple(next_to)].set(top_value)


def level_of(rng, extent, cuts, low, top_value):
    def one(position, blocks):
        draws = jax.random.uniform(jax.random.fold_in(jax.random.fold_in(rng, 6), position), (blocks,), jnp.float32, low / len(cuts), top_value / len(cuts))
        return jnp.repeat(jnp.exp(draws), extent[position] // blocks).reshape((-1,) + (1,) * (len(extent) - position - 1))

    factor_of = one(*cuts[0])
    for cut in cuts[1:]:
        factor_of = factor_of * one(*cut)
    return factor_of


def cumulative_ranks(count, skew):
    weights = [(1 << 20) // math.isqrt(rank ** skew) + 1 for rank in range(1, count + 1)]
    width = 1 + sum(weights) // (1 << 30)
    return np.cumsum(np.array([max(1, weight // width) for weight in weights]))


def skewed_ids(own_key, shape, amount, skew):
    listing = cumulative_ranks(amount, skew)
    lot = jax.random.randint(jax.random.fold_in(own_key, 1), shape, 0, int(listing[amount - 1]))
    rank = jnp.searchsorted(jnp.asarray(listing, jnp.int32), lot, side="right")
    return jax.random.permutation(jax.random.fold_in(own_key, 2), amount)[rank].astype(jnp.int32)


def length_profile(count, total, most, skew):
    portions = [(1 << 20) // math.isqrt(standing ** skew) + 1 for standing in range(2, count + 1)]
    surplus, holding = total - most - (count - 1), [1] * (count - 1)
    while surplus > 0:
        free = [i for i in range(count - 1) if holding[i] < most]
        whole, remaining = sum([portions[i] for i in free]), surplus
        for i in free:
            more = min(most - holding[i], max(1, remaining * portions[i] // whole), surplus)
            holding[i] = holding[i] + more
            surplus = surplus - more
    return np.array([most] + holding)


def ragged_sizes(own_key, number_of, total, reach, skew):
    if number_of == 2:
        one = jax.random.randint(own_key, (), max(1, total - reach), min(reach, total - 1) + 1)
        return jnp.stack([one, total - one])
    sizes = jnp.asarray(length_profile(number_of, total, reach, skew), jnp.int32)
    twos = (number_of - 1) // 2
    giver, sink = sizes[1:1 + 2 * twos:2], sizes[2:2 + 2 * twos:2]
    room = jnp.minimum(giver - 1, reach - sink)
    shifted = jax.random.randint(jax.random.fold_in(own_key, 1), (twos,), 0, 1 << 20) % (room + 1)
    sizes = sizes.at[1:1 + 2 * twos:2].set(giver - shifted).at[2:2 + 2 * twos:2].set(sink + shifted)
    return sizes[jax.random.permutation(jax.random.fold_in(own_key, 2), number_of)]


def assign_block(key, own, number, rows, number_of, top, most, skew):
    order = jax.random.permutation(key, number_of)
    heavy_load, common = portions_of(number_of, rows * top, most, skew, True), portions_of(number_of, rows * top, most, skew, False)
    places = jnp.arange(number_of)

    def named(tallies, turn):
        used = int((tallies > 0).sum())
        fixed = max(1, used // 4)
        shifted = fixed + (places - fixed + turn * (used - fixed)) % max(1, number_of - fixed)
        return jnp.zeros((number_of,), jnp.int32).at[order[jnp.where(places < fixed, places, shifted)]].set(jnp.asarray(tallies, jnp.int32))

    tallies = jnp.where(number % 4 == 0, named(heavy_load, number // 4), named(common, number - number // 4 - 1))
    mixed = jax.random.permutation(jax.random.fold_in(own, 3), number_of)
    donor, sink = mixed[0:number_of // 2 * 2:2], mixed[1:number_of // 2 * 2:2]
    room = jnp.minimum(tallies[donor] - 1, most - tallies[sink]) // 2
    room = jnp.where((donor == order[0]) | (sink == order[0]) | (tallies[sink] == 0), 0, jnp.maximum(room, 0))
    shifted = jax.random.randint(jax.random.fold_in(own, 4), (number_of // 2,), 0, 1 << 20) % (room + 1)
    tallies = tallies.at[donor].add(-shifted).at[sink].add(shifted)
    labels = jnp.searchsorted(jnp.cumsum(tallies), jnp.arange(rows * top), side="right").astype(jnp.int32)
    listing = labels.reshape(top, rows).T
    listing = listing[jax.random.permutation(jax.random.fold_in(own, 1), rows)]
    turn = jax.random.randint(jax.random.fold_in(own, 2), (rows, 1), 0, top)
    return jnp.take_along_axis(listing, (jnp.arange(top)[None, :] + turn) % top, axis=1)


def portions_of(number_of, total, most, skew, full):
    portions = [(1 << 20) // math.isqrt(grade ** skew) + 1 for grade in range(1, number_of + 1)]
    largest = most if full else min(most, max(-(-total // number_of), total * portions[0] // sum(portions)))
    least = 1 if total - largest >= number_of - 1 else 0
    given, spare = [largest] + [least] * (number_of - 1), total - largest - least * (number_of - 1)
    while spare > 0:
        free = [i for i in range(1, number_of) if given[i] < largest] or [i for i in range(1, number_of) if given[i] < most]
        whole, left = sum([portions[i] for i in free]), spare
        for i in free:
            addition = min(most - given[i], max(1, left * portions[i] // whole), spare)
            given[i] = given[i] + addition
            spare = spare - addition
    return np.array(given)


def centred(own_key, extent, width, limit, shards=(), kind=jnp.bfloat16):
    level = level_of(own_key, extent, shards, -0.22, 0.18) if shards else 1.0
    values = jax.random.normal(own_key, extent, jnp.float32) * width * level
    return jnp.minimum(jnp.maximum(values, -limit), limit).astype(kind)


def setup_inputs(seed: int = 0) -> dict:
    key_of = jax.random.split(jax.random.key(seed), 11)
    embed_table = centred(key_of[0], (ROWS_ALL, D), 1.0, 6.0, ((0, 32),))
    adam_m = centred(key_of[1], (ROWS_ALL, D), 0.1, 0.6, ((0, 32),), jnp.float32)
    adam_v = jnp.clip(jnp.exp(math.log(0.03) - 2.3025851 * jax.random.uniform(key_of[2], (ROWS_ALL, D), jnp.float32) ** level_of(key_of[2], (ROWS_ALL, D), ((0, 32),), -0.2, 0.2)), 0.003, 0.03)
    lengths = jax.vmap(lambda own: ragged_sizes(own, HIST, GROUP_TOK, GROUP_TOK // 2, 2))(jax.random.split(key_of[3], N_GROUP)).reshape((N_GROUP, HIST)).astype(jnp.int32)
    row_owner_keys = jax.random.split(jax.random.fold_in(key_of[4], 1), TOTAL_TOK // TOK_DEV)
    row_owner_turns = jax.random.permutation(jax.random.fold_in(key_of[4], 3), TOTAL_TOK // TOK_DEV)
    row_owner = jax.vmap(lambda own, number: assign_block(jax.random.fold_in(key_of[4], 2), own, number, TOK_DEV, N_GROUP, 1, CAP, 2))(row_owner_keys, row_owner_turns).reshape((TOTAL_TOK, 1))
    row_index = set_ends(skewed_ids(key_of[5], (TOTAL_TOK,), TROWS, 2), jax.random.fold_in(key_of[5], 3), 0, TROWS - 1).astype(jnp.int32)
    proj_weight = centred(key_of[6], (D, HEADS * 4 * DH), D ** -0.5, 0.1875, ((1, 8),))
    out_weight = centred(key_of[7], (VDIM, D), VDIM ** -0.5, 0.1875)
    norm_gain = jnp.clip(1.0 + 0.18 * jax.random.normal(key_of[8], (VDIM,), jnp.float32), 0.1, 1.9)
    upstream = centred(key_of[9], (TOTAL_TOK, D), 1.0, 6.0, ((0, 256),))
    return {"embed_table": embed_table, "adam_m": adam_m, "adam_v": adam_v, "lengths": lengths, "row_owner": row_owner, "row_index": row_index, "proj_weight": proj_weight, "out_weight": out_weight, "norm_gain": norm_gain, "upstream": upstream}


learn_rate = 0.05
beta_first = 0.9
beta_second = 0.999
adam_eps = 1e-08
norm_eps = 1e-05
bias_first = 1.0 - 0.9 ** 10
bias_second = 1.0 - 0.999 ** 10

def silu_pair(scores):
    sigma = jax.nn.sigmoid(scores)
    return (scores * sigma, sigma * (1.0 + scores * (1.0 - sigma)))

def norm_rows(attended, gain):
    center_val = lax.optimization_barrier(jnp.mean(attended, axis=-1, keepdims=True))
    centered = attended - center_val
    spread = lax.optimization_barrier(jnp.mean(centered * centered, axis=-1, keepdims=True))
    return centered * lax.rsqrt(spread + norm_eps) * gain

def finish(embedded, attended, units, norm_gain, out_weight, upstream):
    normed, pullback = jax.vjp(lambda inner: norm_rows(inner, norm_gain), attended.astype(jnp.float32))
    unit_vals = units.astype(jnp.float32)
    mixed = (normed * unit_vals).astype(jnp.bfloat16)
    layer_out = embedded.astype(jnp.float32) + jnp.dot(mixed, out_weight, preferred_element_type=jnp.float32)
    d_mixed = jnp.dot(upstream, out_weight.T, preferred_element_type=jnp.float32)
    d_units = (d_mixed * normed).astype(jnp.bfloat16)
    d_attended = pullback(d_mixed * unit_vals)[0].astype(jnp.bfloat16)
    return (layer_out, d_units, d_attended)

def history_ids(group_lengths, group_tok):
    ends = jnp.cumsum(group_lengths)
    places = jnp.arange(group_tok, dtype=jnp.int32)
    return lax.optimization_barrier(jnp.sum((places[:, None] >= ends[None, :]).astype(jnp.int32), axis=1))

def adam_update(embed_table, adam_m, adam_v, row_grad):
    new_moment = beta_first * adam_m + (1.0 - beta_first) * row_grad
    new_second = beta_second * adam_v + (1.0 - beta_second) * row_grad * row_grad
    step_size = new_moment / bias_first / (jnp.sqrt(new_second / bias_second) + adam_eps)
    new_table = embed_table.astype(jnp.float32) - learn_rate * step_size
    return (new_table, new_moment, new_second)

def reference(embed_table, adam_m, adam_v, lengths, row_owner, row_index, proj_weight, out_weight, norm_gain, upstream):
    group_tok = TOK_DEV * N_SEQ
    score_scale = DH ** (-0.5)
    flat_ids = (row_owner[:, 0] * TROWS + row_index).astype(jnp.int32)
    ids_grouped = flat_ids.reshape(N_GROUP, group_tok)
    upstream_grouped = upstream.reshape(N_GROUP, group_tok, D)
    places = jnp.arange(group_tok, dtype=jnp.int32)

    def one_group(row_sum, inputs):
        group_ids, group_lengths, upstream_group = inputs
        embedded = jnp.take(embed_table, group_ids, axis=0)
        pre = jnp.dot(embedded, proj_weight, preferred_element_type=jnp.float32)
        activated, slope_pre = silu_pair(pre)
        proj = activated.astype(jnp.bfloat16).reshape(group_tok, HEADS, 4, DH)
        history = history_ids(group_lengths, group_tok)
        visible = (history[:, None] == history[None, :]) & (places[None, :] <= places[:, None])
        per_head = jnp.transpose(proj, (1, 0, 2, 3))

        def head_forward(parts):
            scores = score_scale * jnp.dot(parts[:, 0], parts[:, 1].T, preferred_element_type=jnp.float32)
            weights = jnp.where(visible, silu_pair(scores)[0], 0.0).astype(jnp.bfloat16)
            return jnp.dot(weights, parts[:, 2], preferred_element_type=jnp.float32).astype(jnp.bfloat16)
        attended = lax.map(head_forward, per_head)
        attended = jnp.transpose(attended, (1, 0, 2)).reshape(group_tok, VDIM)
        units = proj[:, :, 3].reshape(group_tok, VDIM)
        layer_rows, d_units, d_attended = finish(embedded, attended, units, norm_gain, out_weight, upstream_group)
        d_heads = jnp.transpose(d_attended.reshape(group_tok, HEADS, DH), (1, 0, 2))

        def head_backward(inputs_head):
            parts, d_out = inputs_head
            query_part = parts[:, 0]
            key_part = parts[:, 1]
            value_part = parts[:, 2]
            scores = score_scale * jnp.dot(query_part, key_part.T, preferred_element_type=jnp.float32)
            activated_s, slope = silu_pair(scores)
            weights = jnp.where(visible, activated_s, 0.0).astype(jnp.bfloat16)
            d_weights = jnp.dot(d_out, value_part.T, preferred_element_type=jnp.float32)
            d_scores = jnp.where(visible, d_weights * slope, 0.0).astype(jnp.bfloat16)
            d_query = (score_scale * jnp.dot(d_scores, key_part, preferred_element_type=jnp.float32)).astype(jnp.bfloat16)
            d_key = (score_scale * jnp.dot(d_scores.T, query_part, preferred_element_type=jnp.float32)).astype(jnp.bfloat16)
            d_value = jnp.dot(weights.T, d_out, preferred_element_type=jnp.float32).astype(jnp.bfloat16)
            return jnp.stack((d_query, d_key, d_value), axis=1)
        d_qkv = lax.map(head_backward, (per_head, d_heads))
        d_qkv = jnp.transpose(d_qkv, (1, 0, 2, 3))
        d_proj = jnp.concatenate((d_qkv, d_units.reshape(group_tok, HEADS, 1, DH)), axis=2)
        d_proj = d_proj.reshape(group_tok, HEADS * 4 * DH)
        d_pre = (d_proj.astype(jnp.float32) * slope_pre).astype(jnp.bfloat16)
        d_embedded = upstream_group.astype(jnp.float32) + jnp.dot(d_pre, proj_weight.T, preferred_element_type=jnp.float32)
        row_sum = row_sum + jax.ops.segment_sum(d_embedded, group_ids, num_segments=N_GROUP * TROWS)
        return (row_sum, layer_rows)
    row_zeros = jnp.zeros((N_GROUP * TROWS, D), jnp.float32)
    row_grad, layer_blocks = lax.scan(one_group, row_zeros, (ids_grouped, lengths, upstream_grouped))
    layer_out = layer_blocks.reshape(N_GROUP * group_tok, D)
    new_table, new_moment, new_second = adam_update(embed_table, adam_m, adam_v, row_grad)
    return (layer_out, new_table, new_moment, new_second)
```

```python
import functools

import jax
import jax.numpy as jnp
from jax import lax
from jax.experimental import pallas as pl
from jax.experimental.pallas import tpu as pltpu
from jax.sharding import PartitionSpec as P

DH = 64
PAIR = 2 * DH
SCALE = DH ** (-0.5)

learn_rate = 0.05
beta_first = 0.9
beta_second = 0.999
adam_eps = 1e-08
norm_eps = 1e-05
bias_first = 1.0 - 0.9**10
bias_second = 1.0 - 0.999**10

BF = jnp.bfloat16
F32 = jnp.float32
BLOCK = 256
NT = (((1,), (1,)), ((), ()))
TN = (((0,), (0,)), ((), ()))


def mm(a, b, dims=(((1,), (0,)), ((), ()))):
    return lax.dot_general(a, b, dims, preferred_element_type=F32)


def sigmoid(v):
    return 0.5 * jnp.tanh(0.5 * v) + 0.5


def silu_pair(v):
    sigma = sigmoid(v)
    act = v * sigma
    return act, sigma + act * (1.0 - sigma)


def ends_of(len_ref):
    e0 = len_ref[0, 0]
    e1 = e0 + len_ref[0, 1]
    e2 = e1 + len_ref[0, 2]
    return e0, e1, e2


def start_at(i, ends):
    e0, e1, e2 = ends
    return jnp.where(i >= e2, e2, jnp.where(i >= e1, e1, jnp.where(i >= e0, e0, 0)))


def stop_at(i, ends, total):
    e0, e1, e2 = ends
    return jnp.where(i >= e2, total, jnp.where(i >= e1, e2, jnp.where(i >= e0, e1, e0)))


def by_head(x):
    lane = lax.broadcasted_iota(jnp.int32, x.shape, 1)
    zero = jnp.zeros_like(x)
    return jnp.concatenate([jnp.where(lane < DH, x, zero), jnp.where(lane < DH, zero, x)], axis=0)


def merge_heads(x):
    half = x.shape[0] // 2
    lane = lax.broadcasted_iota(jnp.int32, (half, x.shape[1]), 1)
    return jnp.where(lane < DH, x[:half], x[half:])


def attend_kernel(len_ref, qkv_ref, out_ref):
    tokens = qkv_ref.shape[0]
    ends = ends_of(len_ref)

    @pl.loop(0, tokens // BLOCK)
    def _(qb):
        q0 = qb * BLOCK
        qs = by_head(qkv_ref[pl.ds(q0, BLOCK), 0:PAIR]) * jnp.asarray(SCALE, BF)
        row = lax.broadcasted_iota(jnp.int32, (2 * BLOCK, 1), 0)
        i = q0 + jnp.where(row >= BLOCK, row - BLOCK, row)
        start_i = start_at(i, ends)

        def step(kb, acc):
            k0 = kb * BLOCK
            k = qkv_ref[pl.ds(k0, BLOCK), PAIR : 2 * PAIR]
            v = qkv_ref[pl.ds(k0, BLOCK), 2 * PAIR : 3 * PAIR]
            s = mm(qs, k, NT)
            j = k0 + lax.broadcasted_iota(jnp.int32, s.shape, 1)
            visible = (j >= start_i) & (j <= i)
            w = jnp.where(visible, s * sigmoid(s), 0.0).astype(BF)
            return acc + mm(w, v)

        first = lax.div(start_at(q0, ends), BLOCK)
        acc = lax.fori_loop(first, qb + 1, step, jnp.zeros((2 * BLOCK, PAIR), F32))
        out_ref[pl.ds(q0, BLOCK), :] = merge_heads(acc).astype(BF)


def attend_back_kernel(len_ref, qkv_ref, pre_ref, do_ref, out_ref, dq_ref):
    tokens = qkv_ref.shape[0]
    ends = ends_of(len_ref)
    dq_ref[...] = jnp.zeros_like(dq_ref)

    def finish_part(rows, part, d_part):
        slope = silu_pair(pre_ref[rows, part * PAIR : (part + 1) * PAIR])[1]
        out_ref[rows, part * PAIR : (part + 1) * PAIR] = (d_part.astype(BF).astype(F32) * slope).astype(BF)

    @pl.loop(0, tokens // BLOCK)
    def _(kb):
        k0 = kb * BLOCK
        rows = pl.ds(k0, BLOCK)
        k = qkv_ref[rows, PAIR : 2 * PAIR]
        v = qkv_ref[rows, 2 * PAIR : 3 * PAIR]

        def step(qb, carry):
            dk, dv = carry
            q0 = qb * BLOCK
            qs = by_head(qkv_ref[pl.ds(q0, BLOCK), 0:PAIR]) * jnp.asarray(SCALE, BF)
            dos = by_head(do_ref[pl.ds(q0, BLOCK), :])
            s = mm(k, qs, NT)
            dw = mm(v, dos, NT)
            act, slope = silu_pair(s)
            col = lax.broadcasted_iota(jnp.int32, (1, 2 * BLOCK), 1)
            i = q0 + jnp.where(col >= BLOCK, col - BLOCK, col)
            start_i = start_at(i, ends)
            j = k0 + lax.broadcasted_iota(jnp.int32, s.shape, 0)
            visible = (j >= start_i) & (j <= i)
            w = jnp.where(visible, act, 0.0).astype(BF)
            ds = jnp.where(visible, dw * slope, 0.0).astype(BF)
            dq = mm(ds, k, TN)
            dq_ref[pl.ds(q0, BLOCK), :] += merge_heads(dq)
            return dk + mm(ds, qs), dv + mm(w, dos)

        last = lax.div(stop_at(k0 + BLOCK - 1, ends, tokens) - 1, BLOCK)
        zero = jnp.zeros((BLOCK, PAIR), F32)
        dk, dv = lax.fori_loop(kb, last + 1, step, (zero, zero))
        finish_part(rows, 0, dq_ref[rows, :] * SCALE)
        finish_part(rows, 1, dk)
        finish_part(rows, 2, dv)


def finish_kernel(att_ref, emb_ref, wu_ref, wo_ref, gain_ref, up_ref, layer_ref, datt_ref, dpu_ref):
    seq = wu_ref.shape[0]
    emb = emb_ref[...]
    d_mixed = mm(up_ref[...], wo_ref[...], NT)
    x = att_ref[...].astype(F32)
    center = x - jnp.mean(x, axis=-1, keepdims=True)
    spread = jnp.mean(center * center, axis=-1, keepdims=True)
    r = lax.rsqrt(spread + norm_eps)
    xhat = center * r
    gain = gain_ref[...]
    normed = xhat * gain
    pre_u = jnp.concatenate([mm(emb, wu_ref[s]) for s in range(seq)], axis=1)
    act_u, slope_u = silu_pair(pre_u)
    u = act_u.astype(BF).astype(F32)
    mixed = (normed * u).astype(BF)
    layer_ref[...] = emb.astype(F32) + mm(mixed, wo_ref[...])
    dpu_ref[...] = ((d_mixed * normed).astype(BF).astype(F32) * slope_u).astype(BF)
    gx = d_mixed * u * gain
    datt = r * (
        gx
        - jnp.mean(gx, axis=-1, keepdims=True)
        - xhat * jnp.mean(gx * xhat, axis=-1, keepdims=True)
    )
    datt_ref[...] = datt.astype(BF)


def d_embed_kernel(pos_ref, dqkv_ref, dpu_ref, w_ref, up_ref, out_ref):
    seq = w_ref.shape[0]
    d_emb = up_ref[...].astype(F32)
    for s in range(seq):
        d_emb = d_emb + mm(dqkv_ref[s], w_ref[s][:, : 3 * PAIR], NT)
        d_emb = d_emb + mm(dpu_ref[:, s * PAIR : (s + 1) * PAIR], w_ref[s][:, 3 * PAIR :], NT)
    slots = out_ref.shape[0]
    slot = lax.broadcasted_iota(jnp.int32, (slots, pos_ref.shape[1]), 0)
    place = jnp.where(slot == pos_ref[...], 1.0, 0.0).astype(BF)
    out_ref[...] = mm(place, d_emb.astype(BF)).astype(BF)


VM = pl.BlockSpec(memory_space=pltpu.VMEM)
SM = pl.BlockSpec(memory_space=pltpu.SMEM)
MIB = 1 << 20


def local_call(kernel, out_shape, specs, scratch=(), limit=40):
    return pl.pallas_call(
        kernel,
        out_shape=out_shape,
        in_specs=specs,
        out_specs=jax.tree.map(lambda _: VM, out_shape),
        scratch_shapes=list(scratch),
        compiler_params=pltpu.CompilerParams(vmem_limit_bytes=limit * MIB),
    )


def sds(shape, dtype):
    return jax.ShapeDtypeStruct(shape, dtype)


def adam_update(embed_table, adam_m, adam_v, row_grad):
    new_moment = beta_first * adam_m + (1.0 - beta_first) * row_grad
    new_second = beta_second * adam_v + (1.0 - beta_second) * row_grad * row_grad
    step_size = new_moment / bias_first / (jnp.sqrt(new_second / bias_second) + adam_eps)
    new_table = embed_table.astype(F32) - learn_rate * step_size
    return (new_table, new_moment, new_second)


def body(
    embed_table,
    adam_m,
    adam_v,
    lengths,
    row_owner,
    row_index,
    proj_weight,
    out_weight,
    norm_gain,
    upstream,
):
    tok_rows = row_index.shape[0]
    groups = lax.axis_size("group")
    seq = lax.axis_size("seq")
    capacity = 2 * tok_rows // groups
    slots = groups * capacity
    tokens = tok_rows * seq
    width = embed_table.shape[1]
    table_rows = embed_table.shape[0]

    col = jnp.arange(4 * PAIR, dtype=jnp.int32)
    source = (col % PAIR) // DH * (4 * DH) + col // PAIR * DH + col % DH
    shuffle = (jnp.arange(4 * PAIR, dtype=jnp.int32)[:, None] == source[None, :]).astype(BF)
    w_own = jnp.dot(proj_weight, shuffle, preferred_element_type=F32).astype(BF)
    w_all = lax.all_gather(w_own, "seq", axis=0)

    owner = row_owner[:, 0]
    hits = (owner[:, None] == jnp.arange(groups, dtype=jnp.int32)[None, :]).astype(BF)
    before = (jnp.arange(tok_rows)[:, None] > jnp.arange(tok_rows)[None, :]).astype(BF)
    ranks = jnp.dot(before, hits, preferred_element_type=F32)
    slot = jnp.sum(ranks * hits.astype(F32), axis=1).astype(jnp.int32)
    pos = owner * capacity + slot
    place = (jnp.arange(slots, dtype=jnp.int32)[:, None] == pos[None, :]).astype(BF)
    requests = jnp.sum(place.astype(F32) * (row_index + 1).astype(F32)[None, :], axis=1)
    asked = lax.all_to_all(
        requests.astype(jnp.int32).reshape(groups, capacity), "group", split_axis=0, concat_axis=0, tiled=True
    ).reshape(slots) - 1
    wanted = (asked[:, None] == jnp.arange(table_rows, dtype=jnp.int32)[None, :]).astype(BF)
    found = jnp.dot(wanted, embed_table, preferred_element_type=F32).astype(BF)
    returned = lax.all_to_all(
        found.reshape(groups, capacity, width), "group", split_axis=0, concat_axis=0, tiled=True
    ).reshape(slots, width)
    embedded = lax.dot_general(place, returned, TN, preferred_element_type=F32).astype(BF)

    emb_all = lax.all_gather(embedded, "seq", axis=0, tiled=True)
    pre = jnp.dot(emb_all, w_own[:, : 3 * PAIR], preferred_element_type=F32)
    qkv = silu_pair(pre)[0].astype(BF)

    att_heads = local_call(attend_kernel, sds((tokens, PAIR), BF), [SM, VM])(lengths, qkv)
    attended = lax.all_to_all(att_heads, "seq", split_axis=0, concat_axis=1, tiled=True)
    layer_out, d_att, d_pre_u = local_call(
        finish_kernel,
        (sds((tok_rows, width), F32), sds((tok_rows, width), BF), sds((tok_rows, width), BF)),
        [VM] * 6,
    )(attended, embedded, w_all[:, :, 3 * PAIR :], out_weight, norm_gain.reshape(1, -1), upstream)
    d_heads = lax.all_to_all(d_att, "seq", split_axis=1, concat_axis=0, tiled=True)
    d_pre_heads = local_call(
        attend_back_kernel,
        sds((tokens, 3 * PAIR), BF),
        [SM, VM, VM, VM],
        [pltpu.VMEM((tokens, PAIR), F32)],
    )(lengths, qkv, pre, d_heads)
    d_qkv = lax.all_to_all(
        d_pre_heads.reshape(seq, tok_rows, 3 * PAIR), "seq", split_axis=0, concat_axis=0, tiled=True
    )
    outgoing = local_call(d_embed_kernel, sds((slots, width), BF), [VM] * 5)(
        pos.reshape(1, -1), d_qkv, d_pre_u, w_all, upstream
    )
    incoming = lax.all_to_all(
        outgoing.reshape(groups, capacity, width), "group", split_axis=0, concat_axis=0, tiled=True
    ).reshape(slots, width)
    partial = lax.dot_general(wanted, incoming, TN, preferred_element_type=F32).astype(BF)
    shares = lax.all_to_all(
        partial.reshape(seq, table_rows // seq, width), "seq", split_axis=0, concat_axis=0, tiled=True
    )
    share = jnp.sum(shares.astype(F32), axis=0).astype(BF)
    row_grad = lax.all_gather(share, "seq", axis=0, tiled=True).astype(F32)
    new_table, new_moment, new_second = adam_update(embed_table, adam_m, adam_v, row_grad)
    return (layer_out, new_table, new_moment, new_second)


def solution(mesh):
    placed = (
        P("group", None),
        P("group", None),
        P("group", None),
        P("group", None),
        P(("group", "seq"), None),
        P(("group", "seq")),
        P(None, "seq"),
        P(),
        P(),
        P(("group", "seq"), None),
    )
    return jax.shard_map(
        body,
        mesh=mesh,
        in_specs=placed,
        out_specs=(P(("group", "seq"), None), P("group", None), P("group", None), P("group", None)),
        check_vma=False,
    )
```

```python
import functools

import jax
import jax.numpy as jnp
from jax import lax
from jax.experimental import pallas as pl
from jax.experimental.pallas import tpu as pltpu
from jax.sharding import PartitionSpec as P

DH = 64
PAIR = 2 * DH
SCALE = DH ** (-0.5)

learn_rate = 0.05
beta_first = 0.9
beta_second = 0.999
adam_eps = 1e-08
norm_eps = 1e-05
bias_first = 1.0 - 0.9**10
bias_second = 1.0 - 0.999**10

BF = jnp.bfloat16
F32 = jnp.float32
BLOCK = 256
NT = (((1,), (1,)), ((), ()))
TN = (((0,), (0,)), ((), ()))


def mm(a, b, dims=(((1,), (0,)), ((), ()))):
    return lax.dot_general(a, b, dims, preferred_element_type=F32)


def sigmoid(v):
    return 0.5 * jnp.tanh(0.5 * v) + 0.5


def silu_pair(v):
    sigma = sigmoid(v)
    act = v * sigma
    return act, sigma + act * (1.0 - sigma)


def ends_of(len_ref):
    e0 = len_ref[0, 0]
    e1 = e0 + len_ref[0, 1]
    e2 = e1 + len_ref[0, 2]
    return e0, e1, e2


def start_at(i, ends):
    e0, e1, e2 = ends
    return jnp.where(i >= e2, e2, jnp.where(i >= e1, e1, jnp.where(i >= e0, e0, 0)))


def stop_at(i, ends, total):
    e0, e1, e2 = ends
    return jnp.where(i >= e2, total, jnp.where(i >= e1, e2, jnp.where(i >= e0, e1, e0)))


def by_head(x):
    lane = lax.broadcasted_iota(jnp.int32, x.shape, 1)
    zero = jnp.zeros_like(x)
    return jnp.concatenate([jnp.where(lane < DH, x, zero), jnp.where(lane < DH, zero, x)], axis=0)


def merge_heads(x):
    half = x.shape[0] // 2
    lane = lax.broadcasted_iota(jnp.int32, (half, x.shape[1]), 1)
    return jnp.where(lane < DH, x[:half], x[half:])


def attend_kernel(len_ref, qkv_ref, out_ref):
    tokens = qkv_ref.shape[0]
    ends = ends_of(len_ref)

    @pl.loop(0, tokens // BLOCK)
    def _(qb):
        q0 = qb * BLOCK
        qs = by_head(qkv_ref[pl.ds(q0, BLOCK), 0:PAIR]) * jnp.asarray(SCALE, BF)
        row = lax.broadcasted_iota(jnp.int32, (2 * BLOCK, 1), 0)
        i = q0 + jnp.where(row >= BLOCK, row - BLOCK, row)
        start_i = start_at(i, ends)

        def step(kb, acc):
            k0 = kb * BLOCK
            k = qkv_ref[pl.ds(k0, BLOCK), PAIR : 2 * PAIR]
            v = qkv_ref[pl.ds(k0, BLOCK), 2 * PAIR : 3 * PAIR]
            s = mm(qs, k, NT)
            j = k0 + lax.broadcasted_iota(jnp.int32, s.shape, 1)
            visible = (j >= start_i) & (j <= i)
            w = jnp.where(visible, s * sigmoid(s), 0.0).astype(BF)
            return acc + mm(w, v)

        first = lax.div(start_at(q0, ends), BLOCK)
        acc = lax.fori_loop(first, qb + 1, step, jnp.zeros((2 * BLOCK, PAIR), F32))
        out_ref[pl.ds(q0, BLOCK), :] = merge_heads(acc).astype(BF)


def attend_back_kernel(len_ref, qkv_ref, pre_ref, do_ref, out_ref, dq_ref):
    tokens = qkv_ref.shape[0]
    ends = ends_of(len_ref)
    dq_ref[...] = jnp.zeros_like(dq_ref)

    def finish_part(rows, part, d_part):
        slope = silu_pair(pre_ref[rows, part * PAIR : (part + 1) * PAIR])[1]
        out_ref[rows, part * PAIR : (part + 1) * PAIR] = (d_part.astype(BF).astype(F32) * slope).astype(BF)

    @pl.loop(0, tokens // BLOCK)
    def _(kb):
        k0 = kb * BLOCK
        rows = pl.ds(k0, BLOCK)
        k = qkv_ref[rows, PAIR : 2 * PAIR]
        v = qkv_ref[rows, 2 * PAIR : 3 * PAIR]

        def step(qb, carry):
            dk, dv = carry
            q0 = qb * BLOCK
            qs = by_head(qkv_ref[pl.ds(q0, BLOCK), 0:PAIR]) * jnp.asarray(SCALE, BF)
            dos = by_head(do_ref[pl.ds(q0, BLOCK), :])
            s = mm(k, qs, NT)
            dw = mm(v, dos, NT)
            act, slope = silu_pair(s)
            col = lax.broadcasted_iota(jnp.int32, (1, 2 * BLOCK), 1)
            i = q0 + jnp.where(col >= BLOCK, col - BLOCK, col)
            start_i = start_at(i, ends)
            j = k0 + lax.broadcasted_iota(jnp.int32, s.shape, 0)
            visible = (j >= start_i) & (j <= i)
            w = jnp.where(visible, act, 0.0).astype(BF)
            ds = jnp.where(visible, dw * slope, 0.0).astype(BF)
            dq = mm(ds, k, TN)
            dq_ref[pl.ds(q0, BLOCK), :] += merge_heads(dq)
            return dk + mm(ds, qs), dv + mm(w, dos)

        last = lax.div(stop_at(k0 + BLOCK - 1, ends, tokens) - 1, BLOCK)
        zero = jnp.zeros((BLOCK, PAIR), F32)
        dk, dv = lax.fori_loop(kb, last + 1, step, (zero, zero))
        finish_part(rows, 0, dq_ref[rows, :] * SCALE)
        finish_part(rows, 1, dk)
        finish_part(rows, 2, dv)


def shuffle_kernel(w_ref, out_ref):
    size = w_ref.shape[1]
    row = lax.broadcasted_iota(jnp.int32, (size, size), 0)
    col = lax.broadcasted_iota(jnp.int32, (size, size), 1)
    lane = lax.rem(col, PAIR)
    source = lax.div(lane, DH) * (4 * DH) + lax.div(col, PAIR) * DH + lax.rem(lane, DH)
    move = jnp.where(row == source, 1.0, 0.0).astype(BF)
    out_ref[...] = mm(w_ref[...], move).astype(BF)


def group_peers(k, groups):
    depth = min(8, groups)
    lines = groups // depth
    me = lax.axis_index("group")
    y, z = lax.div(me, depth), lax.rem(me, depth)
    dy, dz = lax.div(k, depth), lax.rem(k * 3, depth)
    to = lax.rem(y + dy, lines) * depth + lax.rem(z + dz, depth)
    return to


def seq_peer(k, seq):
    return lax.rem(lax.axis_index("seq") + k, seq)


def send(src, dst, out_sem, in_sem, **where):
    return pltpu.make_async_remote_copy(
        src_ref=src,
        dst_ref=dst,
        send_sem=out_sem,
        recv_sem=in_sem,
        device_id=where,
        device_id_type=pl.DeviceIdType.MESH,
    )


def greet(groups, seq_steps, seq):
    barrier = pltpu.get_barrier_semaphore()

    @pl.loop(1, groups)
    def _(k):
        pl.semaphore_signal(
            barrier, inc=1, device_id={"group": group_peers(k, groups)}, device_id_type=pl.DeviceIdType.MESH
        )

    for peer in seq_steps:
        pl.semaphore_signal(barrier, inc=1, device_id={"seq": peer}, device_id_type=pl.DeviceIdType.MESH)
    return barrier, groups - 1 + len(seq_steps)


def slot_places(owner, slots, groups):
    rows = owner.shape[1]
    hits = lax.broadcasted_iota(jnp.int32, (groups, rows), 0) == owner
    earlier = lax.broadcasted_iota(jnp.int32, (rows, rows), 0) < lax.broadcasted_iota(jnp.int32, (rows, rows), 1)
    count = mm(jnp.where(hits, 1.0, 0.0).astype(BF), jnp.where(earlier, 1.0, 0.0).astype(BF))
    slot = jnp.sum(jnp.where(hits, count, 0.0), axis=0, keepdims=True).astype(jnp.int32)
    pos = owner * (slots // groups) + slot
    return jnp.where(lax.broadcasted_iota(jnp.int32, (slots, rows), 0) == pos, 1.0, 0.0).astype(BF)


def fetch_kernel(
    groups, seq, owner_ref, index_ref, table_ref, w_ref,
    emb_ref, pre_ref, qkv_ref, wanted_ref, place_ref,
    ask_out, ask_in, row_out, row_in, ring, ask_s, ask_r, row_s, row_r, ring_s, ring_r,
):
    chunks, slots, cut = row_out.shape
    rows = owner_ref.shape[1]
    cap = slots // groups
    table_rows = table_ref.shape[0]
    wide = 3 * PAIR
    g, s = lax.axis_index("group"), lax.axis_index("seq")
    chips = seq // 2
    x, core = lax.div(s, 2), lax.rem(s, 2)
    flip = 1 - 2 * core
    right = lax.rem(x + 1, chips) * 2 + core
    left = lax.rem(x + chips - 1, chips) * 2 + core
    across = lax.rem(x + 2, chips) * 2 + core
    sib = s + flip

    barrier, greeted = greet(groups, [sib, right, left], seq)
    place_ref[...] = slot_places(owner_ref[...], slots, groups)
    index = jnp.broadcast_to((index_ref[...] + 1).astype(F32), (PAIR, rows)).astype(BF)
    ask_out[...] = mm(place_ref[...], index, NT).astype(BF)
    pl.semaphore_wait(barrier, greeted)

    mine = pl.ds(pl.multiple_of(g * cap, cap), cap)

    def ask(k):
        to = group_peers(k, groups)
        return send(
            ask_out.at[pl.ds(pl.multiple_of(to * cap, cap), cap)], ask_in.at[mine], ask_s.at[k], ask_r.at[k], group=to
        )

    def give(c, k):
        to = group_peers(k, groups)
        return send(
            row_out.at[c, pl.ds(pl.multiple_of(to * cap, cap), cap)], row_in.at[c, mine],
            row_s.at[c, k], row_r.at[c, k], group=to,
        )

    @pl.loop(1, groups)
    def _(k):
        ask(k).start()

    ask_in[mine] = ask_out[mine]

    @pl.loop(1, groups)
    def _(k):
        ask(k).wait()

    wanted = ask_in[...].astype(F32).astype(jnp.int32)
    for part in range(table_rows // PAIR):
        lane = lax.broadcasted_iota(jnp.int32, wanted.shape, 1) + (part * PAIR + 1)
        wanted_ref[:, part * PAIR : (part + 1) * PAIR] = jnp.where(wanted == lane, 1.0, 0.0).astype(BF)

    for c in range(chunks):
        row_out[c] = mm(wanted_ref[...], table_ref[:, c * cut : (c + 1) * cut]).astype(BF)

        @pl.loop(1, groups)
        def _(k):
            give(c, k).start()

        row_in[c, mine] = row_out[c, mine]

    half = rows // 2

    def hop(c, op, block, to, low=0, size=rows):
        view = ring.at[c, block, pl.ds(low, size)]
        return send(view, view, ring_s.at[c, op], ring_r.at[c, op], seq=to)

    def project(c, block):
        at = pl.ds(pl.multiple_of(block * rows, rows), rows)
        val = mm(ring[c, block], w_ref[c * cut : (c + 1) * cut, :wide])
        if c > 0:
            val = val + pre_ref[at]
        pre_ref[at] = val
        if c == chunks - 1:
            qkv_ref[at] = silu_pair(val)[0].astype(BF)

    for c in range(chunks):

        @pl.loop(1, groups)
        def _(k):
            give(c, k).wait()

        block = mm(place_ref[...], row_in[c], TN).astype(BF)
        emb_ref[:, c * cut : (c + 1) * cut] = block
        ring[c, s] = block
        hop(c, 1, s, right).start()
        hop(c, 2, s, left).start()
        hop(c, 0, s, sib).start()
        project(c, s)
        hop(c, 1, left, right).wait_recv()
        hop(c, 3, left, right, 0, half).start()
        hop(c, 4, left, sib).start()
        hop(c, 2, right, left).wait_recv()
        hop(c, 5, right, left, half, half).start()
        hop(c, 6, right, sib).start()
        project(c, left)
        project(c, right)
        hop(c, 0, sib, sib).wait_recv()
        project(c, sib)
        hop(c, 3, across, right, 0, half).wait_recv()
        hop(c, 7, across, sib, 0, half).start()
        hop(c, 5, across, left, half, half).wait_recv()
        hop(c, 8, across, sib, half, half).start()
        project(c, across)
        hop(c, 4, left + flip, sib).wait_recv()
        project(c, left + flip)
        hop(c, 6, right + flip, sib).wait_recv()
        project(c, right + flip)
        hop(c, 7, across + flip, sib, 0, half).wait_recv()
        hop(c, 8, across + flip, sib, half, half).wait_recv()
        project(c, across + flip)

    for c in range(chunks):
        hop(c, 1, s, right).wait_send()
        hop(c, 2, s, left).wait_send()
        hop(c, 0, s, sib).wait_send()
        hop(c, 3, left, right, 0, half).wait_send()
        hop(c, 4, left, sib).wait_send()
        hop(c, 5, right, left, half, half).wait_send()
        hop(c, 6, right, sib).wait_send()
        hop(c, 7, across, sib, 0, half).wait_send()
        hop(c, 8, across, sib, half, half).wait_send()


def middle_kernel(
    seq, att_ref, emb_ref, w_ref, wo_ref, gain_ref, up_ref,
    layer_ref, dheads_ref, dpu_ref,
    wu, att_in, datt_out, datt_in, d_mixed, pre_u, w_s, att_s, att_r, datt_s, datt_r,
):
    rows, width = emb_ref.shape
    s = lax.axis_index("seq")
    order = [4, 3, 5, 2, 6, 1, 7]

    def load(b):
        return pltpu.make_async_copy(
            w_ref.at[pl.ds(b * width, width), 3 * PAIR : 4 * PAIR], wu.at[b], w_s.at[b]
        )

    for b in range(seq):
        load(b).start()
    barrier, greeted = greet(1, [seq_peer(k, seq) for k in range(1, seq)], seq)
    pl.semaphore_wait(barrier, greeted)

    def hand(k):
        to = seq_peer(k, seq)
        return send(
            att_ref.at[pl.ds(pl.multiple_of(to * rows, rows), rows)], att_in.at[s], att_s.at[k], att_r.at[k], seq=to
        )

    def back(k):
        to = seq_peer(k, seq)
        return send(datt_out.at[to], datt_in.at[s], datt_s.at[k], datt_r.at[k], seq=to)

    for k in order:
        hand(k).start()
    att_in[s] = att_ref[pl.ds(pl.multiple_of(s * rows, rows), rows)]
    d_mixed[...] = mm(up_ref[...], wo_ref[...], NT)
    emb = emb_ref[...]
    for b in range(seq):
        load(b).wait()
        pre_u[:, b * PAIR : (b + 1) * PAIR] = mm(emb, wu[b])
    for k in order:
        hand(k).wait()

    att = jnp.concatenate([att_in[b] for b in range(seq)], axis=1).astype(F32)
    center = att - jnp.mean(att, axis=-1, keepdims=True)
    spread = jnp.mean(center * center, axis=-1, keepdims=True)
    r = lax.rsqrt(spread + norm_eps)
    xhat = center * r
    gain = gain_ref[...]
    normed = xhat * gain
    act_u, slope_u = silu_pair(pre_u[...])
    u = act_u.astype(BF).astype(F32)
    d_mix = d_mixed[...]
    gx = d_mix * u * gain
    datt = r * (
        gx
        - jnp.mean(gx, axis=-1, keepdims=True)
        - xhat * jnp.mean(gx * xhat, axis=-1, keepdims=True)
    )
    datt = datt.astype(BF)
    for b in range(seq):
        datt_out[b] = datt[:, b * PAIR : (b + 1) * PAIR]
    for k in order:
        back(k).start()
    datt_in[s] = datt_out[s]
    dpu = ((d_mix * normed).astype(BF).astype(F32) * slope_u).astype(BF)
    for b in range(seq):
        dpu_ref[b] = dpu[:, b * PAIR : (b + 1) * PAIR]
    mixed = (normed * u).astype(BF)
    layer_ref[...] = emb.astype(F32) + mm(mixed, wo_ref[...])
    for k in order:
        back(k).wait()
    dheads_ref[...] = datt_in[...]


def back_kernel(
    groups, seq, dqkv_ref, dpu_ref, place_ref, wanted_ref, w_ref, up_ref,
    grad_ref,
    w_vm, d_in, row_out, row_in, part, part_f, part_in, share, share_in,
    w_s, d_s, d_r, row_s, row_r, part_s, part_r, share_s, share_r,
):
    chunks, slots, cut = row_out.shape
    rows, width = up_ref.shape
    cap = slots // groups
    wide = 3 * PAIR
    own = grad_ref.shape[0] // seq
    g, s = lax.axis_index("group"), lax.axis_index("seq")
    order = [4, 3, 5, 2, 6, 1, 7]

    def load(b):
        return pltpu.make_async_copy(w_ref.at[pl.ds(b * width, width)], w_vm.at[b], w_s.at[b])

    for b in range(seq):
        load(b).start()
    barrier, greeted = greet(groups, [seq_peer(k, seq) for k in range(1, seq)], seq)
    for b in range(seq):
        d_in[b, :, wide:] = dpu_ref[b]
    d_in[s, :, :wide] = dqkv_ref[pl.ds(pl.multiple_of(s * rows, rows), rows)]
    pl.semaphore_wait(barrier, greeted)

    def hand(k):
        to = seq_peer(k, seq)
        return send(
            dqkv_ref.at[pl.ds(pl.multiple_of(to * rows, rows), rows)], d_in.at[s, :, 0:wide],
            d_s.at[k], d_r.at[k], seq=to,
        )

    mine = pl.ds(pl.multiple_of(g * cap, cap), cap)

    def give(c, k):
        to = group_peers(k, groups)
        return send(
            row_out.at[c, pl.ds(pl.multiple_of(to * cap, cap), cap)], row_in.at[c, mine],
            row_s.at[c, k], row_r.at[c, k], group=to,
        )

    def spread(c, k):
        to = seq_peer(k, seq)
        return send(part.at[c, to], part_in.at[c, s], part_s.at[c, k], part_r.at[c, k], seq=to)

    def copy_share(c, k):
        to = seq_peer(k, seq)
        return send(share.at[c], share_in.at[c, s], share_s.at[c, k], share_r.at[c, k], seq=to)

    for k in order:
        hand(k).start()
    for b in range(seq):
        load(b).wait()

    for c in range(chunks):
        cols = slice(c * cut, (c + 1) * cut)
        total = up_ref[:, cols].astype(F32)
        for k in [0, 7, 1, 6, 2, 5, 3, 4]:
            b = lax.rem(s + seq - k, seq)
            if c == 0 and k > 0:
                hand(k).wait_recv()
            total = total + mm(d_in[b], w_vm[b, cols, :], NT)
        row_out[c] = mm(place_ref[...], total.astype(BF)).astype(BF)

        @pl.loop(1, groups)
        def _(k):
            give(c, k).start()

        row_in[c, mine] = row_out[c, mine]

    for c in range(chunks):

        @pl.loop(1, groups)
        def _(k):
            give(c, k).wait()

        sums = mm(wanted_ref[...], row_in[c], TN)
        for b in range(seq):
            part[c, b] = sums[b * own : (b + 1) * own].astype(BF)
            part_f[b] = sums[b * own : (b + 1) * own]
        for k in order:
            spread(c, k).start()
        total = part_f[s]
        for k in range(1, seq):
            spread(c, k).wait_recv()
            total = total + part_in[c, lax.rem(s + seq - k, seq)].astype(F32)
        share[c] = total
        for k in order:
            copy_share(c, k).start()
        share_in[c, s] = total

    for c in range(chunks):
        for k in order:
            copy_share(c, k).wait()
        for b in range(seq):
            grad_ref[b * own : (b + 1) * own, c * cut : (c + 1) * cut] = share_in[c, b]
        for k in order:
            spread(c, k).wait_send()
    for k in order:
        hand(k).wait_send()


VM = pl.BlockSpec(memory_space=pltpu.VMEM)
SM = pl.BlockSpec(memory_space=pltpu.SMEM)
MIB = 1 << 20


def local_call(kernel, out_shape, specs, scratch=(), limit=40):
    return pl.pallas_call(
        kernel,
        out_shape=out_shape,
        in_specs=specs,
        out_specs=jax.tree.map(lambda _: VM, out_shape),
        scratch_shapes=list(scratch),
        compiler_params=pltpu.CompilerParams(vmem_limit_bytes=limit * MIB),
    )


def remote_call(kernel, ident, out_shape, specs, scratch, limit=48):
    return pl.pallas_call(
        kernel,
        out_shape=out_shape,
        in_specs=specs,
        out_specs=jax.tree.map(lambda _: VM, out_shape),
        scratch_shapes=list(scratch),
        compiler_params=pltpu.CompilerParams(
            collective_id=ident, has_side_effects=True, vmem_limit_bytes=limit * MIB
        ),
    )


ANY = pl.BlockSpec(memory_space=pl.ANY)
CHUNKS = 2
DMA = pltpu.SemaphoreType.DMA


def sds(shape, dtype):
    return jax.ShapeDtypeStruct(shape, dtype)


def adam_update(embed_table, adam_m, adam_v, row_grad):
    new_moment = beta_first * adam_m + (1.0 - beta_first) * row_grad
    new_second = beta_second * adam_v + (1.0 - beta_second) * row_grad * row_grad
    step_size = new_moment / bias_first / (jnp.sqrt(new_second / bias_second) + adam_eps)
    new_table = embed_table.astype(F32) - learn_rate * step_size
    return (new_table, new_moment, new_second)


def body(
    embed_table,
    adam_m,
    adam_v,
    lengths,
    row_owner,
    row_index,
    proj_weight,
    out_weight,
    norm_gain,
    upstream,
):
    tok_rows = row_index.shape[0]
    groups = lax.axis_size("group")
    seq = lax.axis_size("seq")
    capacity = 2 * tok_rows // groups
    slots = groups * capacity
    tokens = tok_rows * seq
    width = embed_table.shape[1]
    table_rows = embed_table.shape[0]

    cut = width // CHUNKS

    w_own = local_call(shuffle_kernel, sds(proj_weight.shape, BF), [VM])(proj_weight)
    w_all = lax.all_gather(w_own, "seq", axis=0, tiled=True)

    embedded, pre, qkv, wanted, place = remote_call(
        functools.partial(fetch_kernel, groups, seq),
        1,
        (
            sds((tok_rows, width), BF),
            sds((tokens, 3 * PAIR), F32),
            sds((tokens, 3 * PAIR), BF),
            sds((slots, table_rows), BF),
            sds((slots, tok_rows), BF),
        ),
        [VM] * 4,
        [
            pltpu.VMEM((slots, PAIR), BF),
            pltpu.VMEM((slots, PAIR), BF),
            pltpu.VMEM((CHUNKS, slots, cut), BF),
            pltpu.VMEM((CHUNKS, slots, cut), BF),
            pltpu.VMEM((CHUNKS, seq, tok_rows, cut), BF),
            DMA((groups,)),
            DMA((groups,)),
            DMA((CHUNKS, groups)),
            DMA((CHUNKS, groups)),
            DMA((CHUNKS, 9)),
            DMA((CHUNKS, 9)),
        ],
    )(row_owner.reshape(1, -1), row_index.reshape(1, -1), embed_table, w_own)

    att_heads = local_call(attend_kernel, sds((tokens, PAIR), BF), [SM, VM])(lengths, qkv)
    layer_out, d_heads, d_pre_u = remote_call(
        functools.partial(middle_kernel, seq),
        2,
        (
            sds((tok_rows, width), F32),
            sds((seq, tok_rows, PAIR), BF),
            sds((seq, tok_rows, PAIR), BF),
        ),
        [VM, VM, ANY, VM, VM, VM],
        [
            pltpu.VMEM((seq, width, PAIR), BF),
            pltpu.VMEM((seq, tok_rows, PAIR), BF),
            pltpu.VMEM((seq, tok_rows, PAIR), BF),
            pltpu.VMEM((seq, tok_rows, PAIR), BF),
            pltpu.VMEM((tok_rows, width), F32),
            pltpu.VMEM((tok_rows, width), F32),
            DMA((seq,)),
            DMA((seq,)),
            DMA((seq,)),
            DMA((seq,)),
            DMA((seq,)),
        ],
    )(att_heads, embedded, w_all, out_weight, norm_gain.reshape(1, -1), upstream)
    d_pre_heads = local_call(
        attend_back_kernel,
        sds((tokens, 3 * PAIR), BF),
        [SM, VM, VM, VM],
        [pltpu.VMEM((tokens, PAIR), F32)],
    )(lengths, qkv, pre, d_heads.reshape(tokens, PAIR))
    own = table_rows // seq
    row_grad = remote_call(
        functools.partial(back_kernel, groups, seq),
        3,
        sds((table_rows, width), F32),
        [VM, VM, VM, VM, ANY, VM],
        [
            pltpu.VMEM((seq, width, 4 * PAIR), BF),
            pltpu.VMEM((seq, tok_rows, 4 * PAIR), BF),
            pltpu.VMEM((CHUNKS, slots, cut), BF),
            pltpu.VMEM((CHUNKS, slots, cut), BF),
            pltpu.VMEM((CHUNKS, seq, own, cut), BF),
            pltpu.VMEM((seq, own, cut), F32),
            pltpu.VMEM((CHUNKS, seq, own, cut), BF),
            pltpu.VMEM((CHUNKS, own, cut), F32),
            pltpu.VMEM((CHUNKS, seq, own, cut), F32),
            DMA((seq,)),
            DMA((seq,)),
            DMA((seq,)),
            DMA((CHUNKS, groups)),
            DMA((CHUNKS, groups)),
            DMA((CHUNKS, seq)),
            DMA((CHUNKS, seq)),
            DMA((CHUNKS, seq)),
            DMA((CHUNKS, seq)),
        ],
    )(d_pre_heads, d_pre_u, place, wanted, w_all, upstream)
    new_table, new_moment, new_second = adam_update(embed_table, adam_m, adam_v, row_grad)
    return (layer_out, new_table, new_moment, new_second)


def solution(mesh):
    placed = (
        P("group", None),
        P("group", None),
        P("group", None),
        P("group", None),
        P(("group", "seq"), None),
        P(("group", "seq")),
        P(None, "seq"),
        P(),
        P(),
        P(("group", "seq"), None),
    )
    return jax.shard_map(
        body,
        mesh=mesh,
        in_specs=placed,
        out_specs=(P(("group", "seq"), None), P("group", None), P("group", None), P("group", None)),
        check_vma=False,
    )
```

```python
import functools

import jax
import jax.numpy as jnp
from jax import lax
from jax.experimental import pallas as pl
from jax.experimental.pallas import tpu as pltpu
from jax.sharding import PartitionSpec as P

DH = 64
PAIR = 2 * DH
SCALE = DH ** (-0.5)

learn_rate = 0.05
beta_first = 0.9
beta_second = 0.999
adam_eps = 1e-08
norm_eps = 1e-05
bias_first = 1.0 - 0.9**10
bias_second = 1.0 - 0.999**10

BF = jnp.bfloat16
F32 = jnp.float32
FWD_Q, FWD_K = 512, 256
BACK_Q, BACK_K = 512, 256
NT = (((1,), (1,)), ((), ()))
TN = (((0,), (0,)), ((), ()))


def mm(a, b, dims=(((1,), (0,)), ((), ()))):
    return lax.dot_general(a, b, dims, preferred_element_type=F32)


def sigmoid(v):
    return 0.5 * jnp.tanh(0.5 * v) + 0.5


def silu_pair(v):
    sigma = sigmoid(v)
    act = v * sigma
    return act, sigma + act * (1.0 - sigma)


def ends_of(len_ref):
    e0 = len_ref[0, 0]
    e1 = e0 + len_ref[0, 1]
    e2 = e1 + len_ref[0, 2]
    return e0, e1, e2


def start_at(i, ends):
    e0, e1, e2 = ends
    return jnp.where(i >= e2, e2, jnp.where(i >= e1, e1, jnp.where(i >= e0, e0, 0)))


def stop_at(i, ends, total):
    e0, e1, e2 = ends
    return jnp.where(i >= e2, total, jnp.where(i >= e1, e2, jnp.where(i >= e0, e1, e0)))


def by_head(x):
    lane = lax.broadcasted_iota(jnp.int32, x.shape, 1)
    zero = jnp.zeros_like(x)
    return jnp.concatenate([jnp.where(lane < DH, x, zero), jnp.where(lane < DH, zero, x)], axis=0)


def merge_heads(x):
    half = x.shape[0] // 2
    lane = lax.broadcasted_iota(jnp.int32, (half, x.shape[1]), 1)
    return jnp.where(lane < DH, x[:half], x[half:])


def attend_kernel(len_ref, qkv_ref, out_ref):
    tokens = qkv_ref.shape[0]
    ends = ends_of(len_ref)

    @pl.loop(0, tokens // FWD_Q)
    def _(qb):
        q0 = qb * FWD_Q
        qs = by_head(qkv_ref[pl.ds(q0, FWD_Q), 0:PAIR]) * jnp.asarray(0.5 * SCALE, BF)
        row = lax.broadcasted_iota(jnp.int32, (2 * FWD_Q, 1), 0)
        i = q0 + jnp.where(row >= FWD_Q, row - FWD_Q, row)
        start_i = start_at(i, ends)

        def step(kb, acc):
            k0 = kb * FWD_K
            k = qkv_ref[pl.ds(k0, FWD_K), PAIR : 2 * PAIR]
            v = qkv_ref[pl.ds(k0, FWD_K), 2 * PAIR : 3 * PAIR]
            h = mm(qs, k, NT)
            j = k0 + lax.broadcasted_iota(jnp.int32, h.shape, 1)
            visible = (j >= start_i) & (j <= i)
            w = jnp.where(visible, h + h * jnp.tanh(h), 0.0).astype(BF)
            return acc + mm(w, v)

        first = lax.div(start_at(q0, ends), FWD_K)
        last = lax.div(q0 + FWD_Q - 1, FWD_K)
        acc = lax.fori_loop(first, last + 1, step, jnp.zeros((2 * FWD_Q, PAIR), F32))
        out_ref[pl.ds(q0, FWD_Q), :] = merge_heads(acc).astype(BF)


def attend_back_kernel(len_ref, qkv_ref, pre_ref, do_ref, out_ref, dq_ref):
    tokens = qkv_ref.shape[0]
    ends = ends_of(len_ref)
    dq_ref[...] = jnp.zeros_like(dq_ref)

    def finish_part(rows, part, d_part):
        slope = silu_pair(pre_ref[rows, part * PAIR : (part + 1) * PAIR])[1]
        out_ref[rows, part * PAIR : (part + 1) * PAIR] = (d_part.astype(BF).astype(F32) * slope).astype(BF)

    @pl.loop(0, tokens // BACK_K)
    def _(kb):
        k0 = kb * BACK_K
        rows = pl.ds(k0, BACK_K)
        k = qkv_ref[rows, PAIR : 2 * PAIR]
        v = qkv_ref[rows, 2 * PAIR : 3 * PAIR] * jnp.asarray(0.5, BF)

        def step(qb, carry):
            dk, dv = carry
            q0 = qb * BACK_Q
            qs = by_head(qkv_ref[pl.ds(q0, BACK_Q), 0:PAIR]) * jnp.asarray(0.5 * SCALE, BF)
            dos = by_head(do_ref[pl.ds(q0, BACK_Q), :])
            h = mm(k, qs, NT)
            dw = mm(v, dos, NT)
            rise = 1.0 + jnp.tanh(h)
            act = h * rise
            slope = rise * ((1.0 + 2.0 * h) - act)
            col = lax.broadcasted_iota(jnp.int32, (1, 2 * BACK_Q), 1)
            i = q0 + jnp.where(col >= BACK_Q, col - BACK_Q, col)
            start_i = start_at(i, ends)
            j = k0 + lax.broadcasted_iota(jnp.int32, h.shape, 0)
            visible = (j >= start_i) & (j <= i)
            w = jnp.where(visible, act, 0.0).astype(BF)
            ds = jnp.where(visible, dw * slope, 0.0).astype(BF)
            dq = mm(ds, k, TN)
            dq_ref[pl.ds(q0, BACK_Q), :] += merge_heads(dq)
            return dk + mm(ds, qs), dv + mm(w, dos)

        first = lax.div(k0, BACK_Q)
        last = lax.div(stop_at(k0 + BACK_K - 1, ends, tokens) - 1, BACK_Q)
        zero = jnp.zeros((BACK_K, PAIR), F32)
        dk, dv = lax.fori_loop(first, last + 1, step, (zero, zero))
        finish_part(rows, 1, dk * 2.0)
        finish_part(rows, 2, dv)

    @pl.loop(0, tokens // BACK_K)
    def _(qb):
        rows = pl.ds(qb * BACK_K, BACK_K)
        finish_part(rows, 0, dq_ref[rows, :] * SCALE)


def by_parts(w):
    size = w.shape[1]
    row = lax.broadcasted_iota(jnp.int32, (size, size), 0)
    col = lax.broadcasted_iota(jnp.int32, (size, size), 1)
    lane = lax.rem(col, PAIR)
    source = lax.div(lane, DH) * (4 * DH) + lax.div(col, PAIR) * DH + lax.rem(lane, DH)
    move = jnp.where(row == source, 1.0, 0.0).astype(BF)
    return mm(w, move).astype(BF)


def group_peers(k, groups):
    depth = min(8, groups)
    lines = groups // depth
    me = lax.axis_index("group")
    y, z = lax.div(me, depth), lax.rem(me, depth)
    dy, dz = lax.div(k, depth), lax.rem(k * 3, depth)
    to = lax.rem(y + dy, lines) * depth + lax.rem(z + dz, depth)
    return to


def seq_peer(k, seq):
    return lax.rem(lax.axis_index("seq") + k, seq)


def send(src, dst, out_sem, in_sem, **where):
    return pltpu.make_async_remote_copy(
        src_ref=src,
        dst_ref=dst,
        send_sem=out_sem,
        recv_sem=in_sem,
        device_id=where,
        device_id_type=pl.DeviceIdType.MESH,
    )


def greet(groups, seq_steps, seq):
    barrier = pltpu.get_barrier_semaphore()

    @pl.loop(1, groups)
    def _(k):
        pl.semaphore_signal(
            barrier, inc=1, device_id={"group": group_peers(k, groups)}, device_id_type=pl.DeviceIdType.MESH
        )

    for peer in seq_steps:
        pl.semaphore_signal(barrier, inc=1, device_id={"seq": peer}, device_id_type=pl.DeviceIdType.MESH)
    return barrier, groups - 1 + len(seq_steps)


def slot_places(owner, slots, groups):
    rows = owner.shape[1]
    hits = lax.broadcasted_iota(jnp.int32, (groups, rows), 0) == owner
    earlier = lax.broadcasted_iota(jnp.int32, (rows, rows), 0) < lax.broadcasted_iota(jnp.int32, (rows, rows), 1)
    count = mm(jnp.where(hits, 1.0, 0.0).astype(BF), jnp.where(earlier, 1.0, 0.0).astype(BF))
    slot = jnp.sum(jnp.where(hits, count, 0.0), axis=0, keepdims=True).astype(jnp.int32)
    pos = owner * (slots // groups) + slot
    return jnp.where(lax.broadcasted_iota(jnp.int32, (slots, rows), 0) == pos, 1.0, 0.0).astype(BF)


def fetch_kernel(
    groups, seq, names_ref, table_ref, w_ref,
    emb_ref, pre_ref, qkv_ref, wanted_ref, place_ref, w_all,
    w_own, table, load_s, w_s, w_r, ask_out, ask_in, row_out, row_in, ring, ask_s, ask_r, row_s, row_r, ring_s, ring_r,
):
    chunks, slots, cut = row_out.shape
    rows = names_ref.shape[1]
    cap = slots // groups
    table_rows, width = table_ref.shape
    wide = 3 * PAIR
    parts = w_s.shape[0]
    deep = width // parts
    g, s = lax.axis_index("group"), lax.axis_index("seq")
    chips = seq // 2
    x, core = lax.div(s, 2), lax.rem(s, 2)
    flip = 1 - 2 * core
    right = lax.rem(x + 1, chips) * 2 + core
    left = lax.rem(x + chips - 1, chips) * 2 + core
    across = lax.rem(x + 2, chips) * 2 + core
    sib = s + flip

    load_w = pltpu.make_async_copy(w_ref, w_own, load_s.at[0])
    load_table = pltpu.make_async_copy(table_ref, table, load_s.at[1])
    load_w.start()
    load_table.start()
    barrier, greeted = greet(groups, [sib, right, left], seq)
    place_ref[...] = slot_places(names_ref[0:1], slots, groups)
    index = jnp.broadcast_to((names_ref[1:2] + 1).astype(F32), (PAIR, rows)).astype(BF)
    ask_out[...] = mm(place_ref[...], index, NT).astype(BF)
    load_w.wait()
    for j in range(parts):
        w_own[j * deep : (j + 1) * deep] = by_parts(w_own[j * deep : (j + 1) * deep])
    keep_w = pltpu.make_async_copy(w_own, w_all.at[pl.ds(pl.multiple_of(s * width, width), width)], load_s.at[2])
    keep_w.start()
    pl.semaphore_wait(barrier, greeted)

    def w_hop(j, op, block, to, low=0, size=deep):
        at = pl.ds(pl.multiple_of(block * width + j * deep + low, size), size)
        src = w_own.at[pl.ds(j * deep, deep)] if op < 3 else w_all.at[at]
        return send(src, w_all.at[at], w_s.at[j, op], w_r.at[j, op], seq=to)

    mine = pl.ds(pl.multiple_of(g * cap, cap), cap)

    def ask(k):
        to = group_peers(k, groups)
        return send(
            ask_out.at[pl.ds(pl.multiple_of(to * cap, cap), cap)], ask_in.at[mine], ask_s.at[k], ask_r.at[k], group=to
        )

    def give(c, k):
        to = group_peers(k, groups)
        return send(
            row_out.at[c, pl.ds(pl.multiple_of(to * cap, cap), cap)], row_in.at[c, mine],
            row_s.at[c, k], row_r.at[c, k], group=to,
        )

    @pl.loop(1, groups)
    def _(k):
        ask(k).start()

    for j in range(parts):
        w_hop(j, 1, s, right).start()
        w_hop(j, 2, s, left).start()
        w_hop(j, 0, s, sib).start()
    ask_in[mine] = ask_out[mine]

    @pl.loop(1, groups)
    def _(k):
        ask(k).wait()

    wanted = ask_in[...].astype(F32).astype(jnp.int32)
    for part in range(table_rows // PAIR):
        lane = lax.broadcasted_iota(jnp.int32, wanted.shape, 1) + (part * PAIR + 1)
        wanted_ref[:, part * PAIR : (part + 1) * PAIR] = jnp.where(wanted == lane, 1.0, 0.0).astype(BF)

    load_table.wait()
    for c in range(chunks):
        row_out[c] = mm(wanted_ref[...], table[:, c * cut : (c + 1) * cut]).astype(BF)

        @pl.loop(1, groups)
        def _(k):
            if c > 0:
                give(c - 1, k).wait_send()
            give(c, k).start()

        row_in[c, mine] = row_out[c, mine]

    half = rows // 2

    def hop(c, op, block, to, low=0, size=rows):
        view = ring.at[c, block, pl.ds(low, size)]
        return send(view, view, ring_s.at[c, op], ring_r.at[c, op], seq=to)

    def project(c, block):
        at = pl.ds(pl.multiple_of(block * rows, rows), rows)
        val = mm(ring[c, block], w_own[c * cut : (c + 1) * cut, :wide])
        if c > 0:
            val = val + pre_ref[at]
        pre_ref[at] = val
        if c == chunks - 1:
            qkv_ref[at] = silu_pair(val)[0].astype(BF)

    def gathered(c):
        @pl.loop(1, groups)
        def _(k):
            give(c, k).wait_recv()
            if c == chunks - 1:
                give(c, k).wait_send()

        block = mm(place_ref[...], row_in[c], TN).astype(BF)
        emb_ref[:, c * cut : (c + 1) * cut] = block
        ring[c, s] = block
        hop(c, 1, s, right).start()
        hop(c, 2, s, left).start()
        hop(c, 0, s, sib).start()
        project(c, s)

    def first_hop(c):
        hop(c, 1, left, right).wait_recv()
        hop(c, 3, left, right, 0, half).start()
        hop(c, 4, left, sib).start()
        hop(c, 2, right, left).wait_recv()
        hop(c, 5, right, left, half, half).start()
        hop(c, 6, right, sib).start()
        project(c, left)
        project(c, right)
        hop(c, 0, sib, sib).wait_recv()
        project(c, sib)

    def second_hop(c):
        hop(c, 3, across, right, 0, half).wait_recv()
        hop(c, 7, across, sib, 0, half).start()
        hop(c, 5, across, left, half, half).wait_recv()
        hop(c, 8, across, sib, half, half).start()
        project(c, across)

    def from_sibling(c):
        hop(c, 4, left + flip, sib).wait_recv()
        project(c, left + flip)
        hop(c, 6, right + flip, sib).wait_recv()
        project(c, right + flip)
        hop(c, 7, across + flip, sib, 0, half).wait_recv()
        hop(c, 8, across + flip, sib, half, half).wait_recv()
        project(c, across + flip)

    for c in range(chunks):
        gathered(c)
        if c == 0:
            for j in range(parts):
                w_hop(j, 1, left, right).wait_recv()
                w_hop(j, 3, left, right, 0, deep // 2).start()
                w_hop(j, 4, left, sib).start()
                w_hop(j, 2, right, left).wait_recv()
                w_hop(j, 5, right, left, deep // 2, deep // 2).start()
                w_hop(j, 6, right, sib).start()
        if c > 0:
            second_hop(c - 1)
        first_hop(c)
        if c > 0:
            from_sibling(c - 1)
    second_hop(chunks - 1)
    from_sibling(chunks - 1)

    for j in range(parts):
        w_hop(j, 3, across, right, 0, deep // 2).wait_recv()
        w_hop(j, 7, across, sib, 0, deep // 2).start()
        w_hop(j, 5, across, left, deep // 2, deep // 2).wait_recv()
        w_hop(j, 8, across, sib, deep // 2, deep // 2).start()
    for j in range(parts):
        w_hop(j, 0, sib, sib).wait_recv()
        w_hop(j, 4, left + flip, sib).wait_recv()
        w_hop(j, 6, right + flip, sib).wait_recv()
        w_hop(j, 7, across + flip, sib, 0, deep // 2).wait_recv()
        w_hop(j, 8, across + flip, sib, deep // 2, deep // 2).wait_recv()
        w_hop(j, 0, s, sib).wait_send()
        w_hop(j, 1, s, right).wait_send()
        w_hop(j, 2, s, left).wait_send()
        w_hop(j, 3, left, right, 0, deep // 2).wait_send()
        w_hop(j, 4, left, sib).wait_send()
        w_hop(j, 5, right, left, deep // 2, deep // 2).wait_send()
        w_hop(j, 6, right, sib).wait_send()
        w_hop(j, 7, across, sib, 0, deep // 2).wait_send()
        w_hop(j, 8, across, sib, deep // 2, deep // 2).wait_send()
    keep_w.wait()
    for c in range(chunks):
        hop(c, 1, s, right).wait_send()
        hop(c, 2, s, left).wait_send()
        hop(c, 0, s, sib).wait_send()
        hop(c, 3, left, right, 0, half).wait_send()
        hop(c, 4, left, sib).wait_send()
        hop(c, 5, right, left, half, half).wait_send()
        hop(c, 6, right, sib).wait_send()
        hop(c, 7, across, sib, 0, half).wait_send()
        hop(c, 8, across, sib, half, half).wait_send()


def middle_kernel(
    seq, att_ref, emb_ref, w_ref, wo_ref, gain_ref, up_ref,
    layer_ref, dheads_ref, dpu_ref,
    wu, wo, mixed, att_in, datt_out, datt_in, d_mixed, pre_u, w_s, wo_s, att_s, att_r, datt_s, datt_r,
):
    rows, width = emb_ref.shape
    s = lax.axis_index("seq")
    order = [4, 3, 5, 2, 6, 1, 7]

    def load(b):
        return pltpu.make_async_copy(
            w_ref.at[pl.ds(b * width, width), 3 * PAIR : 4 * PAIR], wu.at[b], w_s.at[b]
        )

    load_wo = pltpu.make_async_copy(wo_ref, wo, wo_s)
    load_wo.start()
    for b in range(seq):
        load(b).start()
    barrier, greeted = greet(1, [seq_peer(k, seq) for k in range(1, seq)], seq)
    pl.semaphore_wait(barrier, greeted)

    half = rows // HALVES

    def hand(h, k):
        to = seq_peer(k, seq)
        return send(
            att_ref.at[pl.ds(pl.multiple_of(to * rows + h * half, half), half)],
            att_in.at[s, h * half : (h + 1) * half], att_s.at[h, k], att_r.at[h, k], seq=to,
        )

    def back(h, k):
        to = seq_peer(k, seq)
        part = slice(h * half, (h + 1) * half)
        return send(datt_out.at[to, part], datt_in.at[s, part], datt_s.at[h, k], datt_r.at[h, k], seq=to)

    for h in range(HALVES):
        for k in order:
            hand(h, k).start()
    att_in[s] = att_ref[pl.ds(pl.multiple_of(s * rows, rows), rows)]
    load_wo.wait()
    d_mixed[...] = mm(up_ref[...], wo[...], NT)
    emb = emb_ref[...]
    for b in range(seq):
        load(b).wait()
        pre_u[:, b * PAIR : (b + 1) * PAIR] = mm(emb, wu[b])
    gain = gain_ref[...]
    for h in range(HALVES):
        part = slice(h * half, (h + 1) * half)
        for k in order:
            hand(h, k).wait_recv()
        att = jnp.concatenate([att_in[b, part] for b in range(seq)], axis=1).astype(F32)
        center = att - jnp.mean(att, axis=-1, keepdims=True)
        spread = jnp.mean(center * center, axis=-1, keepdims=True)
        r = lax.rsqrt(spread + norm_eps)
        xhat = center * r
        act_u, slope_u = silu_pair(pre_u[part])
        u = act_u.astype(BF).astype(F32)
        d_mix = d_mixed[part]
        gx = d_mix * u * gain
        datt = r * (
            gx
            - jnp.mean(gx, axis=-1, keepdims=True)
            - xhat * jnp.mean(gx * xhat, axis=-1, keepdims=True)
        )
        datt = datt.astype(BF)
        for b in range(seq):
            datt_out[b, part] = datt[:, b * PAIR : (b + 1) * PAIR]
        for k in order:
            back(h, k).start()
        normed = xhat * gain
        dpu = ((d_mix * normed).astype(BF).astype(F32) * slope_u).astype(BF)
        for b in range(seq):
            dpu_ref[b, part] = dpu[:, b * PAIR : (b + 1) * PAIR]
        mixed[part] = (normed * u).astype(BF)
    datt_in[s] = datt_out[s]
    layer_ref[...] = emb.astype(F32) + mm(mixed[...], wo[...])
    for h in range(HALVES):
        for k in order:
            hand(h, k).wait_send()
            back(h, k).wait()
    dheads_ref[...] = datt_in[...]


def back_kernel(
    groups, seq, dqkv_ref, dpu_ref, place_ref, wanted_ref, w_ref, up_ref,
    grad_ref,
    w_vm, d_in, row_out, row_in, part, part_f, part_in, share, share_in,
    w_s, d_s, d_r, row_s, row_r, part_s, part_r, share_s, share_r,
):
    chunks, slots, cut = row_out.shape
    rows, width = up_ref.shape
    cap = slots // groups
    wide = 3 * PAIR
    own = grad_ref.shape[0] // seq
    g, s = lax.axis_index("group"), lax.axis_index("seq")
    order = [4, 3, 5, 2, 6, 1, 7]

    def load(b):
        return pltpu.make_async_copy(w_ref.at[pl.ds(b * width, width)], w_vm.at[b], w_s.at[b])

    for b in range(seq):
        load(b).start()
    barrier, greeted = greet(groups, [seq_peer(k, seq) for k in range(1, seq)], seq)
    for b in range(seq):
        d_in[b, :, wide:] = dpu_ref[b]
    d_in[s, :, :wide] = dqkv_ref[pl.ds(pl.multiple_of(s * rows, rows), rows)]
    pl.semaphore_wait(barrier, greeted)

    def hand(k):
        to = seq_peer(k, seq)
        return send(
            dqkv_ref.at[pl.ds(pl.multiple_of(to * rows, rows), rows)], d_in.at[s, :, 0:wide],
            d_s.at[k], d_r.at[k], seq=to,
        )

    mine = pl.ds(pl.multiple_of(g * cap, cap), cap)

    def give(c, k):
        to = group_peers(k, groups)
        return send(
            row_out.at[c, pl.ds(pl.multiple_of(to * cap, cap), cap)], row_in.at[c, mine],
            row_s.at[c, k], row_r.at[c, k], group=to,
        )

    def spread(c, k):
        to = seq_peer(k, seq)
        return send(part.at[c, to], part_in.at[c, s], part_s.at[c, k], part_r.at[c, k], seq=to)

    x, core = lax.div(s, 2), lax.rem(s, 2)
    sib = s + 1 - 2 * core
    chips = seq // 2

    def copy_share(c, dx):
        to = sib if dx == 0 else lax.rem(x + dx, chips) * 2 + core
        return send(share.at[c], share_in.at[c, s], share_s.at[c, dx], share_r.at[c, dx], seq=to)

    def pass_share(c, dx):
        block = lax.rem(x + chips - dx, chips) * 2 + core
        view = share_in.at[c, block]
        return send(view, view, share_s.at[c, chips + dx], share_r.at[c, chips + dx], seq=sib)

    for k in order:
        hand(k).start()
    for b in range(seq):
        load(b).wait()

    for c in range(chunks):
        cols = slice(c * cut, (c + 1) * cut)
        total = up_ref[:, cols].astype(F32)
        for k in [0, 7, 1, 6, 2, 5, 3, 4]:
            b = lax.rem(s + seq - k, seq)
            if c == 0 and k > 0:
                hand(k).wait_recv()
            total = total + mm(d_in[b], w_vm[b, cols, :], NT)
        row_out[c] = mm(place_ref[...], total.astype(BF)).astype(BF)

        @pl.loop(1, groups)
        def _(k):
            if c > 0:
                give(c - 1, k).wait_send()
            give(c, k).start()

        row_in[c, mine] = row_out[c, mine]

    for c in range(chunks):

        @pl.loop(1, groups)
        def _(k):
            give(c, k).wait_recv()
            if c == chunks - 1:
                give(c, k).wait_send()

        sums = mm(wanted_ref[...], row_in[c], TN)
        for b in range(seq):
            part[c, b] = sums[b * own : (b + 1) * own].astype(BF)
            part_f[b] = sums[b * own : (b + 1) * own]
        for k in order:
            spread(c, k).start()
        total = part_f[s]
        for k in range(1, seq):
            spread(c, k).wait_recv()
            total = total + part_in[c, lax.rem(s + seq - k, seq)].astype(F32)
        share[c] = total
        for dx in [2, 1, 3, 0]:
            copy_share(c, dx).start()
        share_in[c, s] = total

    for c in range(chunks):
        for dx in [1, 3, 2]:
            copy_share(c, dx).wait()
            pass_share(c, dx).start()
        copy_share(c, 0).wait()
        for dx in [1, 3, 2]:
            pass_share(c, dx).wait()
        for b in range(seq):
            grad_ref[b * own : (b + 1) * own, c * cut : (c + 1) * cut] = share_in[c, b]
        for k in order:
            spread(c, k).wait_send()
    for k in order:
        hand(k).wait_send()


VM = pl.BlockSpec(memory_space=pltpu.VMEM)
SM = pl.BlockSpec(memory_space=pltpu.SMEM)
MIB = 1 << 20


def local_call(kernel, out_shape, specs, scratch=(), limit=40):
    return pl.pallas_call(
        kernel,
        out_shape=out_shape,
        in_specs=specs,
        out_specs=jax.tree.map(lambda _: VM, out_shape),
        scratch_shapes=list(scratch),
        compiler_params=pltpu.CompilerParams(vmem_limit_bytes=limit * MIB),
    )


def remote_call(kernel, ident, out_shape, specs, scratch, out_specs=None, limit=48):
    return pl.pallas_call(
        kernel,
        out_shape=out_shape,
        in_specs=specs,
        out_specs=out_specs or jax.tree.map(lambda _: VM, out_shape),
        scratch_shapes=list(scratch),
        compiler_params=pltpu.CompilerParams(
            collective_id=ident, has_side_effects=True, vmem_limit_bytes=limit * MIB
        ),
    )


ANY = pl.BlockSpec(memory_space=pl.ANY)
HBM = pl.BlockSpec(memory_space=pltpu.HBM)
CHUNKS = 2
W_PARTS = 2
HALVES = 2
DMA = pltpu.SemaphoreType.DMA


def sds(shape, dtype):
    return jax.ShapeDtypeStruct(shape, dtype)


def adam_update(embed_table, adam_m, adam_v, row_grad):
    new_moment = beta_first * adam_m + (1.0 - beta_first) * row_grad
    new_second = beta_second * adam_v + (1.0 - beta_second) * row_grad * row_grad
    step_size = new_moment / bias_first / (jnp.sqrt(new_second / bias_second) + adam_eps)
    new_table = embed_table.astype(F32) - learn_rate * step_size
    return (new_table, new_moment, new_second)


def body(
    embed_table,
    adam_m,
    adam_v,
    lengths,
    row_owner,
    row_index,
    proj_weight,
    out_weight,
    norm_gain,
    upstream,
):
    tok_rows = row_index.shape[0]
    groups = lax.axis_size("group")
    seq = lax.axis_size("seq")
    capacity = 2 * tok_rows // groups
    slots = groups * capacity
    tokens = tok_rows * seq
    width = embed_table.shape[1]
    table_rows = embed_table.shape[0]

    cut = width // CHUNKS

    embedded, pre, qkv, wanted, place, w_all = remote_call(
        functools.partial(fetch_kernel, groups, seq),
        1,
        (
            sds((tok_rows, width), BF),
            sds((tokens, 3 * PAIR), F32),
            sds((tokens, 3 * PAIR), BF),
            sds((slots, table_rows), BF),
            sds((slots, tok_rows), BF),
            sds((seq * width, 4 * PAIR), BF),
        ),
        [VM, HBM, HBM],
        [
            pltpu.VMEM((width, 4 * PAIR), BF),
            pltpu.VMEM((table_rows, width), BF),
            DMA((3,)),
            DMA((W_PARTS, 9)),
            DMA((W_PARTS, 9)),
            pltpu.VMEM((slots, PAIR), BF),
            pltpu.VMEM((slots, PAIR), BF),
            pltpu.VMEM((CHUNKS, slots, cut), BF),
            pltpu.VMEM((CHUNKS, slots, cut), BF),
            pltpu.VMEM((CHUNKS, seq, tok_rows, cut), BF),
            DMA((groups,)),
            DMA((groups,)),
            DMA((CHUNKS, groups)),
            DMA((CHUNKS, groups)),
            DMA((CHUNKS, 9)),
            DMA((CHUNKS, 9)),
        ],
        (VM,) * 5 + (HBM,),
    )(jnp.stack([row_owner[:, 0], row_index]), embed_table, proj_weight)

    att_heads = local_call(attend_kernel, sds((tokens, PAIR), BF), [SM, VM])(lengths, qkv)
    layer_out, d_heads, d_pre_u = remote_call(
        functools.partial(middle_kernel, seq),
        2,
        (
            sds((tok_rows, width), F32),
            sds((seq, tok_rows, PAIR), BF),
            sds((seq, tok_rows, PAIR), BF),
        ),
        [VM, VM, ANY, ANY, VM, VM],
        [
            pltpu.VMEM((seq, width, PAIR), BF),
            pltpu.VMEM((width, width), BF),
            pltpu.VMEM((tok_rows, width), BF),
            pltpu.VMEM((seq, tok_rows, PAIR), BF),
            pltpu.VMEM((seq, tok_rows, PAIR), BF),
            pltpu.VMEM((seq, tok_rows, PAIR), BF),
            pltpu.VMEM((tok_rows, width), F32),
            pltpu.VMEM((tok_rows, width), F32),
            DMA((seq,)),
            DMA,
            DMA((HALVES, seq)),
            DMA((HALVES, seq)),
            DMA((HALVES, seq)),
            DMA((HALVES, seq)),
        ],
    )(att_heads, embedded, w_all, out_weight, norm_gain.reshape(1, -1), upstream)
    d_pre_heads = local_call(
        attend_back_kernel,
        sds((tokens, 3 * PAIR), BF),
        [SM, VM, VM, VM],
        [pltpu.VMEM((tokens, PAIR), F32)],
    )(lengths, qkv, pre, d_heads.reshape(tokens, PAIR))
    own = table_rows // seq
    row_grad = remote_call(
        functools.partial(back_kernel, groups, seq),
        3,
        sds((table_rows, width), F32),
        [VM, VM, VM, VM, ANY, VM],
        [
            pltpu.VMEM((seq, width, 4 * PAIR), BF),
            pltpu.VMEM((seq, tok_rows, 4 * PAIR), BF),
            pltpu.VMEM((CHUNKS, slots, cut), BF),
            pltpu.VMEM((CHUNKS, slots, cut), BF),
            pltpu.VMEM((CHUNKS, seq, own, cut), BF),
            pltpu.VMEM((seq, own, cut), F32),
            pltpu.VMEM((CHUNKS, seq, own, cut), BF),
            pltpu.VMEM((CHUNKS, own, cut), F32),
            pltpu.VMEM((CHUNKS, seq, own, cut), F32),
            DMA((seq,)),
            DMA((seq,)),
            DMA((seq,)),
            DMA((CHUNKS, groups)),
            DMA((CHUNKS, groups)),
            DMA((CHUNKS, seq)),
            DMA((CHUNKS, seq)),
            DMA((CHUNKS, seq)),
            DMA((CHUNKS, seq)),
        ],
    )(d_pre_heads, d_pre_u, place, wanted, w_all, upstream)
    new_table, new_moment, new_second = adam_update(embed_table, adam_m, adam_v, row_grad)
    return (layer_out, new_table, new_moment, new_second)


def solution(mesh):
    placed = (
        P("group", None),
        P("group", None),
        P("group", None),
        P("group", None),
        P(("group", "seq"), None),
        P(("group", "seq")),
        P(None, "seq"),
        P(),
        P(),
        P(("group", "seq"), None),
    )
    return jax.shard_map(
        body,
        mesh=mesh,
        in_specs=placed,
        out_specs=(P(("group", "seq"), None), P("group", None), P("group", None), P("group", None)),
        check_vma=False,
    )
```

```python
import functools

import jax
import jax.numpy as jnp
from jax import lax
from jax.experimental import pallas as pl
from jax.experimental.pallas import tpu as pltpu
from jax.sharding import PartitionSpec as P

DH = 64
PAIR = 2 * DH
SCALE = DH ** (-0.5)

learn_rate = 0.05
beta_first = 0.9
beta_second = 0.999
adam_eps = 1e-08
norm_eps = 1e-05
bias_first = 1.0 - 0.9**10
bias_second = 1.0 - 0.999**10

BF = jnp.bfloat16
F32 = jnp.float32
FWD_Q, FWD_K = 512, 256
BACK_Q, BACK_K = 512, 256
NT = (((1,), (1,)), ((), ()))
TN = (((0,), (0,)), ((), ()))


def mm(a, b, dims=(((1,), (0,)), ((), ()))):
    return lax.dot_general(a, b, dims, preferred_element_type=F32)


def sigmoid(v):
    return 0.5 * jnp.tanh(0.5 * v) + 0.5


def silu_pair(v):
    sigma = sigmoid(v)
    act = v * sigma
    return act, sigma + act * (1.0 - sigma)


def ends_of(len_ref):
    e0 = len_ref[0, 0]
    e1 = e0 + len_ref[0, 1]
    e2 = e1 + len_ref[0, 2]
    return e0, e1, e2


def start_at(i, ends):
    e0, e1, e2 = ends
    return jnp.where(i >= e2, e2, jnp.where(i >= e1, e1, jnp.where(i >= e0, e0, 0)))


def stop_at(i, ends, total):
    e0, e1, e2 = ends
    return jnp.where(i >= e2, total, jnp.where(i >= e1, e2, jnp.where(i >= e0, e1, e0)))


def by_head(x):
    lane = lax.broadcasted_iota(jnp.int32, x.shape, 1)
    zero = jnp.zeros_like(x)
    return jnp.concatenate([jnp.where(lane < DH, x, zero), jnp.where(lane < DH, zero, x)], axis=0)


def merge_heads(x):
    half = x.shape[0] // 2
    lane = lax.broadcasted_iota(jnp.int32, (half, x.shape[1]), 1)
    return jnp.where(lane < DH, x[:half], x[half:])


def attend_kernel(len_ref, qkv_ref, out_ref):
    tokens = qkv_ref.shape[0]
    ends = ends_of(len_ref)

    @pl.loop(0, tokens // FWD_Q)
    def _(qb):
        q0 = qb * FWD_Q
        qs = by_head(qkv_ref[pl.ds(q0, FWD_Q), 0:PAIR]) * jnp.asarray(0.5 * SCALE, BF)
        row = lax.broadcasted_iota(jnp.int32, (2 * FWD_Q, 1), 0)
        i = q0 + jnp.where(row >= FWD_Q, row - FWD_Q, row)
        start_i = start_at(i, ends)

        def step(kb, acc):
            k0 = kb * FWD_K
            k = qkv_ref[pl.ds(k0, FWD_K), PAIR : 2 * PAIR]
            v = qkv_ref[pl.ds(k0, FWD_K), 2 * PAIR : 3 * PAIR]
            h = mm(qs, k, NT)
            j = k0 + lax.broadcasted_iota(jnp.int32, h.shape, 1)
            visible = (j >= start_i) & (j <= i)
            w = jnp.where(visible, h + h * jnp.tanh(h), 0.0).astype(BF)
            return acc + mm(w, v)

        first = lax.div(start_at(q0, ends), FWD_K)
        last = lax.div(q0 + FWD_Q - 1, FWD_K)
        acc = lax.fori_loop(first, last + 1, step, jnp.zeros((2 * FWD_Q, PAIR), F32))
        out_ref[pl.ds(q0, FWD_Q), :] = merge_heads(acc).astype(BF)


def attend_back_kernel(len_ref, qkv_ref, do_ref, out_ref, dq_ref):
    tokens = qkv_ref.shape[0]
    ends = ends_of(len_ref)
    dq_ref[...] = jnp.zeros_like(dq_ref)

    def finish_part(rows, part, d_part):
        out_ref[rows, part * PAIR : (part + 1) * PAIR] = d_part.astype(BF)

    @pl.loop(0, tokens // BACK_K)
    def _(kb):
        k0 = kb * BACK_K
        rows = pl.ds(k0, BACK_K)
        k = qkv_ref[rows, PAIR : 2 * PAIR]
        v = qkv_ref[rows, 2 * PAIR : 3 * PAIR] * jnp.asarray(0.5, BF)

        def step(qb, carry):
            dk, dv = carry
            q0 = qb * BACK_Q
            qs = by_head(qkv_ref[pl.ds(q0, BACK_Q), 0:PAIR]) * jnp.asarray(0.5 * SCALE, BF)
            dos = by_head(do_ref[pl.ds(q0, BACK_Q), :])
            h = mm(k, qs, NT)
            dw = mm(v, dos, NT)
            rise = 1.0 + jnp.tanh(h)
            act = h * rise
            slope = rise * ((1.0 + 2.0 * h) - act)
            col = lax.broadcasted_iota(jnp.int32, (1, 2 * BACK_Q), 1)
            i = q0 + jnp.where(col >= BACK_Q, col - BACK_Q, col)
            start_i = start_at(i, ends)
            j = k0 + lax.broadcasted_iota(jnp.int32, h.shape, 0)
            visible = (j >= start_i) & (j <= i)
            w = jnp.where(visible, act, 0.0).astype(BF)
            ds = jnp.where(visible, dw * slope, 0.0).astype(BF)
            dq = mm(ds, k, TN)
            dq_ref[pl.ds(q0, BACK_Q), :] += merge_heads(dq)
            return dk + mm(ds, qs), dv + mm(w, dos)

        first = lax.div(k0, BACK_Q)
        last = lax.div(stop_at(k0 + BACK_K - 1, ends, tokens) - 1, BACK_Q)
        zero = jnp.zeros((BACK_K, PAIR), F32)
        dk, dv = lax.fori_loop(first, last + 1, step, (zero, zero))
        finish_part(rows, 1, dk * 2.0)
        finish_part(rows, 2, dv)

    @pl.loop(0, tokens // BACK_K)
    def _(qb):
        rows = pl.ds(qb * BACK_K, BACK_K)
        finish_part(rows, 0, dq_ref[rows, :] * SCALE)


def by_parts(w):
    size = w.shape[1]
    row = lax.broadcasted_iota(jnp.int32, (size, size), 0)
    col = lax.broadcasted_iota(jnp.int32, (size, size), 1)
    lane = lax.rem(col, PAIR)
    source = lax.div(lane, DH) * (4 * DH) + lax.div(col, PAIR) * DH + lax.rem(lane, DH)
    move = jnp.where(row == source, 1.0, 0.0).astype(BF)
    return mm(w, move).astype(BF)


def group_peers(k, groups):
    depth = min(8, groups)
    lines = groups // depth
    me = lax.axis_index("group")
    y, z = lax.div(me, depth), lax.rem(me, depth)
    dy, dz = lax.div(k, depth), lax.rem(k * 5, depth)
    to = lax.rem(y + dy, lines) * depth + lax.rem(z + dz, depth)
    return to


def seq_peer(k, seq):
    return lax.rem(lax.axis_index("seq") + k, seq)


def send(src, dst, out_sem, in_sem, **where):
    return pltpu.make_async_remote_copy(
        src_ref=src,
        dst_ref=dst,
        send_sem=out_sem,
        recv_sem=in_sem,
        device_id=where,
        device_id_type=pl.DeviceIdType.MESH,
    )


def greet(groups, seq_steps, seq):
    barrier = pltpu.get_barrier_semaphore()

    @pl.loop(1, groups)
    def _(k):
        pl.semaphore_signal(
            barrier, inc=1, device_id={"group": group_peers(k, groups)}, device_id_type=pl.DeviceIdType.MESH
        )

    for peer in seq_steps:
        pl.semaphore_signal(barrier, inc=1, device_id={"seq": peer}, device_id_type=pl.DeviceIdType.MESH)
    return barrier, groups - 1 + len(seq_steps)


def slot_places(owner, slots, groups):
    rows = owner.shape[1]
    hits = lax.broadcasted_iota(jnp.int32, (groups, rows), 0) == owner
    earlier = lax.broadcasted_iota(jnp.int32, (rows, rows), 0) < lax.broadcasted_iota(jnp.int32, (rows, rows), 1)
    count = mm(jnp.where(hits, 1.0, 0.0).astype(BF), jnp.where(earlier, 1.0, 0.0).astype(BF))
    slot = jnp.sum(jnp.where(hits, count, 0.0), axis=0, keepdims=True).astype(jnp.int32)
    pos = owner * (slots // groups) + slot
    return jnp.where(lax.broadcasted_iota(jnp.int32, (slots, rows), 0) == pos, 1.0, 0.0).astype(BF)


def fetch_kernel(
    groups, seq, names_ref, table_ref, w_ref,
    emb_ref, slope_ref, pre_u_ref, qkv_ref, wanted_ref, place_ref, w_all,
    w_vm, table, qkv_out, qkv_in, load_s, keep_s, w_s, w_r,
    ask_out, ask_in, row_out, row_in, ask_s, ask_r, row_s, row_r, qkv_s, qkv_r,
):
    chunks, slots, cut = row_out.shape
    rows = names_ref.shape[1]
    cap = slots // groups
    table_rows, width = table_ref.shape
    wide = 3 * PAIR
    half = width // 2
    g, s = lax.axis_index("group"), lax.axis_index("seq")
    chips = seq // 2
    x, core = lax.div(s, 2), lax.rem(s, 2)
    flip = 1 - 2 * core
    right = lax.rem(x + 1, chips) * 2 + core
    left = lax.rem(x + chips - 1, chips) * 2 + core
    across = lax.rem(x + 2, chips) * 2 + core
    sib = s + flip
    order = [4, 3, 5, 2, 6, 1, 7]

    load_w = pltpu.make_async_copy(w_ref, w_vm.at[s], load_s.at[0])
    load_table = pltpu.make_async_copy(table_ref, table, load_s.at[1])
    load_w.start()
    load_table.start()
    barrier, greeted = greet(groups, [seq_peer(k, seq) for k in range(1, seq)], seq)
    place_ref[...] = slot_places(names_ref[0:1], slots, groups)
    index = jnp.broadcast_to((names_ref[1:2] + 1).astype(F32), (PAIR, rows)).astype(BF)
    ask_out[...] = mm(place_ref[...], index, NT).astype(BF)
    load_w.wait()
    for low in (0, half):
        w_vm[s, low : low + half] = by_parts(w_vm[s, low : low + half])
    pl.semaphore_wait(barrier, greeted)

    def w_hop(j, op, block, to, low=0, size=width):
        view = w_vm.at[block, pl.ds(low, size), (wide if j else 0) : (4 * PAIR if j else wide)]
        return send(view, view, w_s.at[j, op], w_r.at[j, op], seq=to)

    def w_start(j):
        w_hop(j, 1, s, right).start()
        w_hop(j, 2, s, left).start()
        w_hop(j, 0, s, sib).start()

    def w_first(j):
        w_hop(j, 1, left, right).wait_recv()
        w_hop(j, 3, left, right, 0, half).start()
        w_hop(j, 4, left, sib).start()
        w_hop(j, 2, right, left).wait_recv()
        w_hop(j, 5, right, left, half, half).start()
        w_hop(j, 6, right, sib).start()

    def w_second(j):
        w_hop(j, 3, across, right, 0, half).wait_recv()
        w_hop(j, 7, across, sib, 0, half).start()
        w_hop(j, 5, across, left, half, half).wait_recv()
        w_hop(j, 8, across, sib, half, half).start()

    def w_last(j):
        w_hop(j, 0, sib, sib).wait_recv()
        w_hop(j, 4, left + flip, sib).wait_recv()
        w_hop(j, 6, right + flip, sib).wait_recv()
        w_hop(j, 7, across + flip, sib, 0, half).wait_recv()
        w_hop(j, 8, across + flip, sib, half, half).wait_recv()

    def w_sent(j):
        w_hop(j, 0, s, sib).wait_send()
        w_hop(j, 1, s, right).wait_send()
        w_hop(j, 2, s, left).wait_send()
        w_hop(j, 3, left, right, 0, half).wait_send()
        w_hop(j, 4, left, sib).wait_send()
        w_hop(j, 5, right, left, half, half).wait_send()
        w_hop(j, 6, right, sib).wait_send()
        w_hop(j, 7, across, sib, 0, half).wait_send()
        w_hop(j, 8, across, sib, half, half).wait_send()

    mine = pl.ds(pl.multiple_of(g * cap, cap), cap)

    def ask(k):
        to = group_peers(k, groups)
        return send(
            ask_out.at[pl.ds(pl.multiple_of(to * cap, cap), cap)], ask_in.at[mine], ask_s.at[k], ask_r.at[k], group=to
        )

    def give(c, k):
        to = group_peers(k, groups)
        return send(
            row_out.at[c, pl.ds(pl.multiple_of(to * cap, cap), cap)], row_in.at[c, mine],
            row_s.at[c, k], row_r.at[c, k], group=to,
        )

    @pl.loop(1, groups)
    def _(k):
        ask(k).start()

    w_start(0)
    ask_in[mine] = ask_out[mine]

    @pl.loop(1, groups)
    def _(k):
        ask(k).wait()

    wanted = ask_in[...].astype(F32).astype(jnp.int32)
    for part in range(table_rows // PAIR):
        lane = lax.broadcasted_iota(jnp.int32, wanted.shape, 1) + (part * PAIR + 1)
        wanted_ref[:, part * PAIR : (part + 1) * PAIR] = jnp.where(wanted == lane, 1.0, 0.0).astype(BF)

    load_table.wait()
    for c in range(chunks):
        row_out[c] = mm(wanted_ref[...], table[:, c * cut : (c + 1) * cut]).astype(BF)

        @pl.loop(1, groups)
        def _(k):
            give(c, k).start()

        row_in[c, mine] = row_out[c, mine]

    def gathered(c):
        @pl.loop(1, groups)
        def _(k):
            give(c, k).wait()

        emb_ref[:, c * cut : (c + 1) * cut] = mm(place_ref[...], row_in[c], TN).astype(BF)

    w_first(0)
    w_start(1)
    w_second(0)
    for c in range(chunks):
        gathered(c)
    w_last(0)
    w_first(1)

    def share(k):
        to = seq_peer(k, seq)
        return send(qkv_out.at[to], qkv_in.at[s], qkv_s.at[k], qkv_r.at[k], seq=to)

    def keep(b):
        return pltpu.make_async_copy(w_vm.at[b], w_all.at[pl.ds(b * width, width)], keep_s.at[b])

    for k in order + [0]:
        to = seq_peer(k, seq)
        act, slope = silu_pair(mm(emb_ref[...], w_vm[to, :, :wide]))
        qkv_out[to] = act.astype(BF)
        slope_ref[to] = slope
        if k > 0:
            share(k).start()
    qkv_in[s] = qkv_out[s]
    w_second(1)
    w_last(1)
    for b in range(seq):
        pre_u_ref[b] = mm(emb_ref[...], w_vm[b, :, wide:])
        keep(b).start()
    w_sent(0)
    w_sent(1)
    for b in range(seq):
        keep(b).wait()
    for k in order:
        share(k).wait()
    for b in range(seq):
        qkv_ref[b * rows : (b + 1) * rows] = qkv_in[b]


def middle_kernel(
    seq, att_ref, emb_ref, pre_u_ref, wo_ref, gain_ref, up_ref,
    layer_ref, dheads_ref, dpu_ref,
    wo, mixed, att_in, datt_out, datt_in, d_mixed, wo_s, att_s, att_r, datt_s, datt_r,
):
    rows, width = emb_ref.shape
    s = lax.axis_index("seq")
    order = [4, 3, 5, 2, 6, 1, 7]

    load_wo = pltpu.make_async_copy(wo_ref, wo, wo_s)
    load_wo.start()
    barrier, greeted = greet(1, [seq_peer(k, seq) for k in range(1, seq)], seq)
    pl.semaphore_wait(barrier, greeted)

    half = rows // HALVES

    def hand(h, k):
        to = seq_peer(k, seq)
        return send(
            att_ref.at[pl.ds(pl.multiple_of(to * rows + h * half, half), half)],
            att_in.at[s, h * half : (h + 1) * half], att_s.at[h, k], att_r.at[h, k], seq=to,
        )

    def back(h, k):
        to = seq_peer(k, seq)
        part = slice(h * half, (h + 1) * half)
        return send(datt_out.at[to, part], datt_in.at[s, part], datt_s.at[h, k], datt_r.at[h, k], seq=to)

    for h in range(HALVES):
        for k in order:
            hand(h, k).start()
    att_in[s] = att_ref[pl.ds(pl.multiple_of(s * rows, rows), rows)]
    load_wo.wait()
    d_mixed[...] = mm(up_ref[...], wo[...], NT)
    emb = emb_ref[...]
    gain = gain_ref[...]
    for h in range(HALVES):
        part = slice(h * half, (h + 1) * half)
        for k in order:
            hand(h, k).wait_recv()
        att = jnp.concatenate([att_in[b, part] for b in range(seq)], axis=1).astype(F32)
        center = att - jnp.mean(att, axis=-1, keepdims=True)
        spread = jnp.mean(center * center, axis=-1, keepdims=True)
        r = lax.rsqrt(spread + norm_eps)
        xhat = center * r
        act_u, slope_u = silu_pair(jnp.concatenate([pre_u_ref[b, part] for b in range(seq)], axis=1))
        u = act_u.astype(BF).astype(F32)
        d_mix = d_mixed[part]
        gx = d_mix * u * gain
        datt = r * (
            gx
            - jnp.mean(gx, axis=-1, keepdims=True)
            - xhat * jnp.mean(gx * xhat, axis=-1, keepdims=True)
        )
        datt = datt.astype(BF)
        for b in range(seq):
            datt_out[b, part] = datt[:, b * PAIR : (b + 1) * PAIR]
        for k in order:
            back(h, k).start()
        normed = xhat * gain
        dpu = ((d_mix * normed).astype(BF).astype(F32) * slope_u).astype(BF)
        for b in range(seq):
            dpu_ref[b, part] = dpu[:, b * PAIR : (b + 1) * PAIR]
        mixed[part] = (normed * u).astype(BF)
    datt_in[s] = datt_out[s]
    layer_ref[...] = emb.astype(F32) + mm(mixed[...], wo[...])
    for h in range(HALVES):
        for k in order:
            hand(h, k).wait_send()
            back(h, k).wait()
    dheads_ref[...] = datt_in[...]


def back_kernel(
    groups, seq, dqkv_ref, dpu_ref, place_ref, wanted_ref, w_ref, slope_ref, up_ref,
    grad_ref,
    w_vm, slope, slope_s, d_in, row_out, row_in, part, part_f, part_in, share, share_in,
    w_s, d_s, d_r, row_s, row_r, part_s, part_r, share_s, share_r,
):
    chunks, slots, cut = row_out.shape
    rows, width = up_ref.shape
    cap = slots // groups
    wide = 3 * PAIR
    own = grad_ref.shape[0] // seq
    g, s = lax.axis_index("group"), lax.axis_index("seq")
    order = [4, 3, 5, 2, 6, 1, 7]

    def load(b):
        return pltpu.make_async_copy(w_ref.at[pl.ds(b * width, width)], w_vm.at[b], w_s.at[b])

    load_slope = pltpu.make_async_copy(slope_ref, slope, slope_s)
    load_slope.start()
    for b in range(seq):
        load(b).start()
    barrier, greeted = greet(groups, [seq_peer(k, seq) for k in range(1, seq)], seq)
    for b in range(seq):
        d_in[b, :, wide:] = dpu_ref[b]
    d_in[s, :, :wide] = dqkv_ref[pl.ds(pl.multiple_of(s * rows, rows), rows)]
    pl.semaphore_wait(barrier, greeted)

    def hand(k):
        to = seq_peer(k, seq)
        return send(
            dqkv_ref.at[pl.ds(pl.multiple_of(to * rows, rows), rows)], d_in.at[s, :, 0:wide],
            d_s.at[k], d_r.at[k], seq=to,
        )

    mine = pl.ds(pl.multiple_of(g * cap, cap), cap)

    def give(c, k):
        to = group_peers(k, groups)
        return send(
            row_out.at[c, pl.ds(pl.multiple_of(to * cap, cap), cap)], row_in.at[c, mine],
            row_s.at[c, k], row_r.at[c, k], group=to,
        )

    def spread(c, k):
        to = seq_peer(k, seq)
        return send(part.at[c, to], part_in.at[c, s], part_s.at[c, k], part_r.at[c, k], seq=to)

    x, core = lax.div(s, 2), lax.rem(s, 2)
    sib = s + 1 - 2 * core
    chips = seq // 2

    def copy_share(c, dx):
        to = sib if dx == 0 else lax.rem(x + dx, chips) * 2 + core
        return send(share.at[c], share_in.at[c, s], share_s.at[c, dx], share_r.at[c, dx], seq=to)

    def pass_share(c, dx):
        block = lax.rem(x + chips - dx, chips) * 2 + core
        view = share_in.at[c, block]
        return send(view, view, share_s.at[c, chips + dx], share_r.at[c, chips + dx], seq=sib)

    for k in order:
        hand(k).start()
    load_slope.wait()
    for b in range(seq):
        load(b).wait()

    for c in range(chunks):
        cols = slice(c * cut, (c + 1) * cut)
        total = up_ref[:, cols].astype(F32)
        for k in [0, 7, 1, 6, 2, 5, 3, 4]:
            b = lax.rem(s + seq - k, seq)
            if c == 0 and k > 0:
                hand(k).wait_recv()
            if c == 0:
                d_in[b, :, :wide] = (d_in[b, :, :wide].astype(F32) * slope[b]).astype(BF)
            total = total + mm(d_in[b], w_vm[b, cols, :], NT)
        row_out[c] = mm(place_ref[...], total.astype(BF)).astype(BF)

        @pl.loop(1, groups)
        def _(k):
            if c > 0:
                give(c - 1, k).wait_send()
            give(c, k).start()

        row_in[c, mine] = row_out[c, mine]

    for c in range(chunks):

        @pl.loop(1, groups)
        def _(k):
            give(c, k).wait_recv()
            if c == chunks - 1:
                give(c, k).wait_send()

        sums = mm(wanted_ref[...], row_in[c], TN)
        for b in range(seq):
            part[c, b] = sums[b * own : (b + 1) * own].astype(BF)
            part_f[b] = sums[b * own : (b + 1) * own]
        for k in order:
            spread(c, k).start()
        total = part_f[s]
        for k in range(1, seq):
            spread(c, k).wait_recv()
            total = total + part_in[c, lax.rem(s + seq - k, seq)].astype(F32)
        share[c] = total
        for dx in [2, 1, 3, 0]:
            copy_share(c, dx).start()
        share_in[c, s] = total

    for c in range(chunks):
        for dx in [1, 3, 2]:
            copy_share(c, dx).wait()
            pass_share(c, dx).start()
        copy_share(c, 0).wait()
        for dx in [1, 3, 2]:
            pass_share(c, dx).wait()
        for b in range(seq):
            grad_ref[b * own : (b + 1) * own, c * cut : (c + 1) * cut] = share_in[c, b]
        for k in order:
            spread(c, k).wait_send()
    for k in order:
        hand(k).wait_send()


VM = pl.BlockSpec(memory_space=pltpu.VMEM)
SM = pl.BlockSpec(memory_space=pltpu.SMEM)
MIB = 1 << 20


def local_call(kernel, out_shape, specs, scratch=(), limit=40):
    return pl.pallas_call(
        kernel,
        out_shape=out_shape,
        in_specs=specs,
        out_specs=jax.tree.map(lambda _: VM, out_shape),
        scratch_shapes=list(scratch),
        compiler_params=pltpu.CompilerParams(vmem_limit_bytes=limit * MIB),
    )


def remote_call(kernel, ident, out_shape, specs, scratch, out_specs=None, limit=48):
    return pl.pallas_call(
        kernel,
        out_shape=out_shape,
        in_specs=specs,
        out_specs=out_specs or jax.tree.map(lambda _: VM, out_shape),
        scratch_shapes=list(scratch),
        compiler_params=pltpu.CompilerParams(
            collective_id=ident, has_side_effects=True, vmem_limit_bytes=limit * MIB
        ),
    )


ANY = pl.BlockSpec(memory_space=pl.ANY)
HBM = pl.BlockSpec(memory_space=pltpu.HBM)
CHUNKS = 2
HALVES = 2
DMA = pltpu.SemaphoreType.DMA


def sds(shape, dtype):
    return jax.ShapeDtypeStruct(shape, dtype)


def adam_update(embed_table, adam_m, adam_v, row_grad):
    new_moment = beta_first * adam_m + (1.0 - beta_first) * row_grad
    new_second = beta_second * adam_v + (1.0 - beta_second) * row_grad * row_grad
    step_size = new_moment / bias_first / (jnp.sqrt(new_second / bias_second) + adam_eps)
    new_table = embed_table.astype(F32) - learn_rate * step_size
    return (new_table, new_moment, new_second)


def body(
    embed_table,
    adam_m,
    adam_v,
    lengths,
    row_owner,
    row_index,
    proj_weight,
    out_weight,
    norm_gain,
    upstream,
):
    tok_rows = row_index.shape[0]
    groups = lax.axis_size("group")
    seq = lax.axis_size("seq")
    capacity = 2 * tok_rows // groups
    slots = groups * capacity
    tokens = tok_rows * seq
    width = embed_table.shape[1]
    table_rows = embed_table.shape[0]

    cut = width // CHUNKS

    embedded, slope, pre_u, qkv, wanted, place, w_all = remote_call(
        functools.partial(fetch_kernel, groups, seq),
        1,
        (
            sds((tok_rows, width), BF),
            sds((seq, tok_rows, 3 * PAIR), F32),
            sds((seq, tok_rows, PAIR), F32),
            sds((tokens, 3 * PAIR), BF),
            sds((slots, table_rows), BF),
            sds((slots, tok_rows), BF),
            sds((seq * width, 4 * PAIR), BF),
        ),
        [VM, HBM, HBM],
        [
            pltpu.VMEM((seq, width, 4 * PAIR), BF),
            pltpu.VMEM((table_rows, width), BF),
            pltpu.VMEM((seq, tok_rows, 3 * PAIR), BF),
            pltpu.VMEM((seq, tok_rows, 3 * PAIR), BF),
            DMA((2,)),
            DMA((seq,)),
            DMA((2, 9)),
            DMA((2, 9)),
            pltpu.VMEM((slots, PAIR), BF),
            pltpu.VMEM((slots, PAIR), BF),
            pltpu.VMEM((CHUNKS, slots, cut), BF),
            pltpu.VMEM((CHUNKS, slots, cut), BF),
            DMA((groups,)),
            DMA((groups,)),
            DMA((CHUNKS, groups)),
            DMA((CHUNKS, groups)),
            DMA((seq,)),
            DMA((seq,)),
        ],
        (VM,) * 6 + (HBM,),
    )(jnp.stack([row_owner[:, 0], row_index]), embed_table, proj_weight)

    att_heads = local_call(attend_kernel, sds((tokens, PAIR), BF), [SM, VM])(lengths, qkv)
    layer_out, d_heads, d_pre_u = remote_call(
        functools.partial(middle_kernel, seq),
        2,
        (
            sds((tok_rows, width), F32),
            sds((seq, tok_rows, PAIR), BF),
            sds((seq, tok_rows, PAIR), BF),
        ),
        [VM, VM, VM, ANY, VM, VM],
        [
            pltpu.VMEM((width, width), BF),
            pltpu.VMEM((tok_rows, width), BF),
            pltpu.VMEM((seq, tok_rows, PAIR), BF),
            pltpu.VMEM((seq, tok_rows, PAIR), BF),
            pltpu.VMEM((seq, tok_rows, PAIR), BF),
            pltpu.VMEM((tok_rows, width), F32),
            DMA,
            DMA((HALVES, seq)),
            DMA((HALVES, seq)),
            DMA((HALVES, seq)),
            DMA((HALVES, seq)),
        ],
    )(att_heads, embedded, pre_u, out_weight, norm_gain.reshape(1, -1), upstream)
    d_qkv_heads = local_call(
        attend_back_kernel,
        sds((tokens, 3 * PAIR), BF),
        [SM, VM, VM],
        [pltpu.VMEM((tokens, PAIR), F32)],
    )(lengths, qkv, d_heads.reshape(tokens, PAIR))
    own = table_rows // seq
    row_grad = remote_call(
        functools.partial(back_kernel, groups, seq),
        3,
        sds((table_rows, width), F32),
        [VM, VM, VM, VM, ANY, ANY, VM],
        [
            pltpu.VMEM((seq, width, 4 * PAIR), BF),
            pltpu.VMEM((seq, tok_rows, 3 * PAIR), F32),
            DMA,
            pltpu.VMEM((seq, tok_rows, 4 * PAIR), BF),
            pltpu.VMEM((CHUNKS, slots, cut), BF),
            pltpu.VMEM((CHUNKS, slots, cut), BF),
            pltpu.VMEM((CHUNKS, seq, own, cut), BF),
            pltpu.VMEM((seq, own, cut), F32),
            pltpu.VMEM((CHUNKS, seq, own, cut), BF),
            pltpu.VMEM((CHUNKS, own, cut), F32),
            pltpu.VMEM((CHUNKS, seq, own, cut), F32),
            DMA((seq,)),
            DMA((seq,)),
            DMA((seq,)),
            DMA((CHUNKS, groups)),
            DMA((CHUNKS, groups)),
            DMA((CHUNKS, seq)),
            DMA((CHUNKS, seq)),
            DMA((CHUNKS, seq)),
            DMA((CHUNKS, seq)),
        ],
    )(d_qkv_heads, d_pre_u, place, wanted, w_all, slope, upstream)
    new_table, new_moment, new_second = adam_update(embed_table, adam_m, adam_v, row_grad)
    return (layer_out, new_table, new_moment, new_second)


def solution(mesh):
    placed = (
        P("group", None),
        P("group", None),
        P("group", None),
        P("group", None),
        P(("group", "seq"), None),
        P(("group", "seq")),
        P(None, "seq"),
        P(),
        P(),
        P(("group", "seq"), None),
    )
    return jax.shard_map(
        body,
        mesh=mesh,
        in_specs=placed,
        out_specs=(P(("group", "seq"), None), P("group", None), P("group", None), P("group", None)),
        check_vma=False,
    )
```

```python
import functools

import jax
import jax.numpy as jnp
from jax import lax
from jax.experimental import pallas as pl
from jax.experimental.pallas import tpu as pltpu
from jax.sharding import PartitionSpec as P

DH = 64
PAIR = 2 * DH
SCALE = DH ** (-0.5)

learn_rate = 0.05
beta_first = 0.9
beta_second = 0.999
adam_eps = 1e-08
norm_eps = 1e-05
bias_first = 1.0 - 0.9**10
bias_second = 1.0 - 0.999**10

BF = jnp.bfloat16
F32 = jnp.float32
FWD_Q, FWD_K = 512, 256
BACK_Q, BACK_K = 512, 256
NT = (((1,), (1,)), ((), ()))
TN = (((0,), (0,)), ((), ()))


def mm(a, b, dims=(((1,), (0,)), ((), ()))):
    return lax.dot_general(a, b, dims, preferred_element_type=F32)


def sigmoid(v):
    return 0.5 * jnp.tanh(0.5 * v) + 0.5


def silu_pair(v):
    sigma = sigmoid(v)
    act = v * sigma
    return act, sigma + act * (1.0 - sigma)


def ends_of(len_ref):
    e0 = len_ref[0, 0]
    e1 = e0 + len_ref[0, 1]
    e2 = e1 + len_ref[0, 2]
    return e0, e1, e2


def start_at(i, ends):
    e0, e1, e2 = ends
    return jnp.where(i >= e2, e2, jnp.where(i >= e1, e1, jnp.where(i >= e0, e0, 0)))


def stop_at(i, ends, total):
    e0, e1, e2 = ends
    return jnp.where(i >= e2, total, jnp.where(i >= e1, e2, jnp.where(i >= e0, e1, e0)))


def by_head(x):
    lane = lax.broadcasted_iota(jnp.int32, x.shape, 1)
    zero = jnp.zeros_like(x)
    return jnp.concatenate([jnp.where(lane < DH, x, zero), jnp.where(lane < DH, zero, x)], axis=0)


def merge_heads(x):
    half = x.shape[0] // 2
    lane = lax.broadcasted_iota(jnp.int32, (half, x.shape[1]), 1)
    return jnp.where(lane < DH, x[:half], x[half:])


def attend_kernel(len_ref, qkv_ref, out_ref):
    tokens = qkv_ref.shape[0]
    ends = ends_of(len_ref)

    @pl.loop(0, tokens // FWD_Q)
    def _(qb):
        q0 = qb * FWD_Q
        qs = by_head(qkv_ref[pl.ds(q0, FWD_Q), 0:PAIR]) * jnp.asarray(0.5 * SCALE, BF)
        row = lax.broadcasted_iota(jnp.int32, (2 * FWD_Q, 1), 0)
        i = q0 + jnp.where(row >= FWD_Q, row - FWD_Q, row)
        start_i = start_at(i, ends)

        def step(kb, acc):
            k0 = kb * FWD_K
            k = qkv_ref[pl.ds(k0, FWD_K), PAIR : 2 * PAIR]
            v = qkv_ref[pl.ds(k0, FWD_K), 2 * PAIR : 3 * PAIR]
            h = mm(qs, k, NT)
            j = k0 + lax.broadcasted_iota(jnp.int32, h.shape, 1)
            visible = (j >= start_i) & (j <= i)
            w = jnp.where(visible, h + h * jnp.tanh(h), 0.0).astype(BF)
            return acc + mm(w, v)

        first = lax.div(start_at(q0, ends), FWD_K)
        last = lax.div(q0 + FWD_Q - 1, FWD_K)
        acc = lax.fori_loop(first, last + 1, step, jnp.zeros((2 * FWD_Q, PAIR), F32))
        out_ref[pl.ds(q0, FWD_Q), :] = merge_heads(acc).astype(BF)


def attend_back_kernel(len_ref, qkv_ref, do_ref, out_ref, dq_ref):
    tokens = qkv_ref.shape[0]
    ends = ends_of(len_ref)
    dq_ref[...] = jnp.zeros_like(dq_ref)

    def finish_part(rows, part, d_part):
        out_ref[rows, part * PAIR : (part + 1) * PAIR] = d_part.astype(BF)

    @pl.loop(0, tokens // BACK_K)
    def _(kb):
        k0 = kb * BACK_K
        rows = pl.ds(k0, BACK_K)
        k = qkv_ref[rows, PAIR : 2 * PAIR]
        v = qkv_ref[rows, 2 * PAIR : 3 * PAIR] * jnp.asarray(0.5, BF)

        def step(qb, carry):
            dk, dv = carry
            q0 = qb * BACK_Q
            qs = by_head(qkv_ref[pl.ds(q0, BACK_Q), 0:PAIR]) * jnp.asarray(0.5 * SCALE, BF)
            dos = by_head(do_ref[pl.ds(q0, BACK_Q), :])
            h = mm(k, qs, NT)
            dw = mm(v, dos, NT)
            rise = 1.0 + jnp.tanh(h)
            act = h * rise
            slope = rise * ((1.0 + 2.0 * h) - act)
            col = lax.broadcasted_iota(jnp.int32, (1, 2 * BACK_Q), 1)
            i = q0 + jnp.where(col >= BACK_Q, col - BACK_Q, col)
            start_i = start_at(i, ends)
            j = k0 + lax.broadcasted_iota(jnp.int32, h.shape, 0)
            visible = (j >= start_i) & (j <= i)
            w = jnp.where(visible, act, 0.0).astype(BF)
            ds = jnp.where(visible, dw * slope, 0.0).astype(BF)
            dq = mm(ds, k, TN)
            dq_ref[pl.ds(q0, BACK_Q), :] += merge_heads(dq)
            return dk + mm(ds, qs), dv + mm(w, dos)

        first = lax.div(k0, BACK_Q)
        last = lax.div(stop_at(k0 + BACK_K - 1, ends, tokens) - 1, BACK_Q)
        zero = jnp.zeros((BACK_K, PAIR), F32)
        dk, dv = lax.fori_loop(first, last + 1, step, (zero, zero))
        finish_part(rows, 1, dk * 2.0)
        finish_part(rows, 2, dv)

    @pl.loop(0, tokens // BACK_K)
    def _(qb):
        rows = pl.ds(qb * BACK_K, BACK_K)
        finish_part(rows, 0, dq_ref[rows, :] * SCALE)


def by_parts(w):
    size = w.shape[1]
    row = lax.broadcasted_iota(jnp.int32, (size, size), 0)
    col = lax.broadcasted_iota(jnp.int32, (size, size), 1)
    lane = lax.rem(col, PAIR)
    source = lax.div(lane, DH) * (4 * DH) + lax.div(col, PAIR) * DH + lax.rem(lane, DH)
    move = jnp.where(row == source, 1.0, 0.0).astype(BF)
    return mm(w, move).astype(BF)


def group_peers(k, groups):
    depth = min(8, groups)
    lines = groups // depth
    me = lax.axis_index("group")
    y, z = lax.div(me, depth), lax.rem(me, depth)
    dy, dz = lax.div(k, depth), lax.rem(k * 5, depth)
    to = lax.rem(y + dy, lines) * depth + lax.rem(z + dz, depth)
    return to


def seq_peer(k, seq):
    return lax.rem(lax.axis_index("seq") + k, seq)


def send(src, dst, out_sem, in_sem, **where):
    return pltpu.make_async_remote_copy(
        src_ref=src,
        dst_ref=dst,
        send_sem=out_sem,
        recv_sem=in_sem,
        device_id=where,
        device_id_type=pl.DeviceIdType.MESH,
    )


def greet(groups, seq_steps, seq):
    barrier = pltpu.get_barrier_semaphore()

    @pl.loop(1, groups)
    def _(k):
        pl.semaphore_signal(
            barrier, inc=1, device_id={"group": group_peers(k, groups)}, device_id_type=pl.DeviceIdType.MESH
        )

    for peer in seq_steps:
        pl.semaphore_signal(barrier, inc=1, device_id={"seq": peer}, device_id_type=pl.DeviceIdType.MESH)
    return barrier, groups - 1 + len(seq_steps)


def slot_places(owner, slots, groups):
    rows = owner.shape[1]
    hits = lax.broadcasted_iota(jnp.int32, (groups, rows), 0) == owner
    earlier = lax.broadcasted_iota(jnp.int32, (rows, rows), 0) < lax.broadcasted_iota(jnp.int32, (rows, rows), 1)
    count = mm(jnp.where(hits, 1.0, 0.0).astype(BF), jnp.where(earlier, 1.0, 0.0).astype(BF))
    slot = jnp.sum(jnp.where(hits, count, 0.0), axis=0, keepdims=True).astype(jnp.int32)
    pos = owner * (slots // groups) + slot
    return jnp.where(lax.broadcasted_iota(jnp.int32, (slots, rows), 0) == pos, 1.0, 0.0).astype(BF)


def fetch_kernel(
    groups, seq, names_ref, table_ref, w_ref,
    emb_ref, slope_ref, pre_u_ref, qkv_ref, wanted_ref, place_ref, w_all,
    w_vm, table, qkv_out, qkv_in, load_s, keep_s, w_s, w_r,
    ask_out, ask_in, row_out, row_in, ask_s, ask_r, row_s, row_r, qkv_s, qkv_r,
):
    chunks, slots, cut = row_out.shape
    rows = names_ref.shape[1]
    cap = slots // groups
    table_rows, width = table_ref.shape
    wide = 3 * PAIR
    half = width // 2
    g, s = lax.axis_index("group"), lax.axis_index("seq")
    chips = seq // 2
    x, core = lax.div(s, 2), lax.rem(s, 2)
    flip = 1 - 2 * core
    right = lax.rem(x + 1, chips) * 2 + core
    left = lax.rem(x + chips - 1, chips) * 2 + core
    across = lax.rem(x + 2, chips) * 2 + core
    sib = s + flip
    order = [4, 3, 5, 2, 6, 1, 7]

    load_w = pltpu.make_async_copy(w_ref, w_vm.at[s], load_s.at[0])
    load_table = pltpu.make_async_copy(table_ref, table, load_s.at[1])
    load_w.start()
    load_table.start()
    barrier, greeted = greet(groups, [seq_peer(k, seq) for k in range(1, seq)], seq)
    place_ref[...] = slot_places(names_ref[0:1], slots, groups)
    index = jnp.broadcast_to((names_ref[1:2] + 1).astype(F32), (PAIR, rows)).astype(BF)
    ask_out[...] = mm(place_ref[...], index, NT).astype(BF)
    load_w.wait()
    for low in (0, half):
        w_vm[s, low : low + half] = by_parts(w_vm[s, low : low + half])
    pl.semaphore_wait(barrier, greeted)

    def w_hop(j, op, block, to, low=0, size=width):
        view = w_vm.at[block, pl.ds(low, size), (wide if j else 0) : (4 * PAIR if j else wide)]
        return send(view, view, w_s.at[j, op], w_r.at[j, op], seq=to)

    def w_start(j):
        w_hop(j, 1, s, right).start()
        w_hop(j, 2, s, left).start()
        w_hop(j, 0, s, sib).start()

    def w_first(j):
        w_hop(j, 1, left, right).wait_recv()
        w_hop(j, 3, left, right, 0, half).start()
        w_hop(j, 4, left, sib).start()
        w_hop(j, 2, right, left).wait_recv()
        w_hop(j, 5, right, left, half, half).start()
        w_hop(j, 6, right, sib).start()

    def w_second(j):
        w_hop(j, 3, across, right, 0, half).wait_recv()
        w_hop(j, 7, across, sib, 0, half).start()
        w_hop(j, 5, across, left, half, half).wait_recv()
        w_hop(j, 8, across, sib, half, half).start()

    def w_last(j):
        w_hop(j, 0, sib, sib).wait_recv()
        w_hop(j, 4, left + flip, sib).wait_recv()
        w_hop(j, 6, right + flip, sib).wait_recv()
        w_hop(j, 7, across + flip, sib, 0, half).wait_recv()
        w_hop(j, 8, across + flip, sib, half, half).wait_recv()

    def w_sent(j):
        w_hop(j, 0, s, sib).wait_send()
        w_hop(j, 1, s, right).wait_send()
        w_hop(j, 2, s, left).wait_send()
        w_hop(j, 3, left, right, 0, half).wait_send()
        w_hop(j, 4, left, sib).wait_send()
        w_hop(j, 5, right, left, half, half).wait_send()
        w_hop(j, 6, right, sib).wait_send()
        w_hop(j, 7, across, sib, 0, half).wait_send()
        w_hop(j, 8, across, sib, half, half).wait_send()

    mine = pl.ds(pl.multiple_of(g * cap, cap), cap)

    def ask(k):
        to = group_peers(k, groups)
        return send(
            ask_out.at[pl.ds(pl.multiple_of(to * cap, cap), cap)], ask_in.at[mine], ask_s.at[k], ask_r.at[k], group=to
        )

    def give(c, k):
        to = group_peers(k, groups)
        return send(
            row_out.at[c, pl.ds(pl.multiple_of(to * cap, cap), cap)], row_in.at[c, mine],
            row_s.at[c, k], row_r.at[c, k], group=to,
        )

    @pl.loop(1, groups)
    def _(k):
        ask(k).start()

    w_start(0)
    ask_in[mine] = ask_out[mine]

    @pl.loop(1, groups)
    def _(k):
        ask(k).wait()

    wanted = ask_in[...].astype(F32).astype(jnp.int32)
    for part in range(table_rows // PAIR):
        lane = lax.broadcasted_iota(jnp.int32, wanted.shape, 1) + (part * PAIR + 1)
        wanted_ref[:, part * PAIR : (part + 1) * PAIR] = jnp.where(wanted == lane, 1.0, 0.0).astype(BF)

    load_table.wait()
    for c in range(chunks):
        row_out[c] = mm(wanted_ref[...], table[:, c * cut : (c + 1) * cut]).astype(BF)

        @pl.loop(1, groups)
        def _(k):
            give(c, k).start()

        row_in[c, mine] = row_out[c, mine]

    def gathered(c):
        @pl.loop(1, groups)
        def _(k):
            give(c, k).wait()

        emb_ref[:, c * cut : (c + 1) * cut] = mm(place_ref[...], row_in[c], TN).astype(BF)

    w_first(0)
    w_start(1)
    w_second(0)
    for c in range(chunks):
        gathered(c)
    w_last(0)
    w_first(1)

    def share(k):
        to = seq_peer(k, seq)
        return send(qkv_out.at[to], qkv_in.at[s], qkv_s.at[k], qkv_r.at[k], seq=to)

    def keep(b):
        return pltpu.make_async_copy(w_vm.at[b], w_all.at[pl.ds(b * width, width)], keep_s.at[b])

    for k in order + [0]:
        to = seq_peer(k, seq)
        act, slope = silu_pair(mm(emb_ref[...], w_vm[to, :, :wide]))
        qkv_out[to] = act.astype(BF)
        slope_ref[to] = slope
        if k > 0:
            share(k).start()
    qkv_in[s] = qkv_out[s]
    w_second(1)
    w_last(1)
    for b in range(seq):
        pre_u_ref[b] = mm(emb_ref[...], w_vm[b, :, wide:])
        keep(b).start()
    w_sent(0)
    w_sent(1)
    for b in range(seq):
        keep(b).wait()
    for k in order:
        share(k).wait()
    for b in range(seq):
        qkv_ref[b * rows : (b + 1) * rows] = qkv_in[b]


def middle_kernel(
    seq, att_ref, emb_ref, pre_u_ref, wo_ref, gain_ref, up_ref,
    layer_ref, dheads_ref, dpu_ref,
    wo, mixed, att_in, datt_out, datt_in, d_mixed, wo_s, att_s, att_r, datt_s, datt_r,
):
    rows, width = emb_ref.shape
    s = lax.axis_index("seq")
    order = [4, 3, 5, 2, 6, 1, 7]

    load_wo = pltpu.make_async_copy(wo_ref, wo, wo_s)
    load_wo.start()
    barrier, greeted = greet(1, [seq_peer(k, seq) for k in range(1, seq)], seq)
    pl.semaphore_wait(barrier, greeted)

    half = rows // HALVES

    def hand(h, k):
        to = seq_peer(k, seq)
        return send(
            att_ref.at[pl.ds(pl.multiple_of(to * rows + h * half, half), half)],
            att_in.at[s, h * half : (h + 1) * half], att_s.at[h, k], att_r.at[h, k], seq=to,
        )

    def back(h, k):
        to = seq_peer(k, seq)
        part = slice(h * half, (h + 1) * half)
        return send(datt_out.at[to, part], datt_in.at[s, part], datt_s.at[h, k], datt_r.at[h, k], seq=to)

    for h in range(HALVES):
        for k in order:
            hand(h, k).start()
    att_in[s] = att_ref[pl.ds(pl.multiple_of(s * rows, rows), rows)]
    load_wo.wait()
    d_mixed[...] = mm(up_ref[...], wo[...], NT)
    emb = emb_ref[...]
    gain = gain_ref[...]
    for h in range(HALVES):
        part = slice(h * half, (h + 1) * half)
        for k in order:
            hand(h, k).wait_recv()
        att = jnp.concatenate([att_in[b, part] for b in range(seq)], axis=1).astype(F32)
        center = att - jnp.mean(att, axis=-1, keepdims=True)
        spread = jnp.mean(center * center, axis=-1, keepdims=True)
        r = lax.rsqrt(spread + norm_eps)
        xhat = center * r
        act_u, slope_u = silu_pair(jnp.concatenate([pre_u_ref[b, part] for b in range(seq)], axis=1))
        u = act_u.astype(BF).astype(F32)
        d_mix = d_mixed[part]
        gx = d_mix * u * gain
        datt = r * (
            gx
            - jnp.mean(gx, axis=-1, keepdims=True)
            - xhat * jnp.mean(gx * xhat, axis=-1, keepdims=True)
        )
        datt = datt.astype(BF)
        for b in range(seq):
            datt_out[b, part] = datt[:, b * PAIR : (b + 1) * PAIR]
        for k in order:
            back(h, k).start()
        normed = xhat * gain
        dpu = ((d_mix * normed).astype(BF).astype(F32) * slope_u).astype(BF)
        for b in range(seq):
            dpu_ref[b, part] = dpu[:, b * PAIR : (b + 1) * PAIR]
        mixed[part] = (normed * u).astype(BF)
    datt_in[s] = datt_out[s]
    layer_ref[...] = emb.astype(F32) + mm(mixed[...], wo[...])
    for h in range(HALVES):
        for k in order:
            hand(h, k).wait_send()
            back(h, k).wait()
    dheads_ref[...] = datt_in[...]


def back_kernel(
    groups, seq, dqkv_ref, dpu_ref, place_ref, wanted_ref, w_ref, slope_ref, up_ref,
    grad_ref,
    w_vm, slope, slope_s, d_in, row_out, row_in, part, part_f, part_in, share, share_in,
    w_s, d_s, d_r, row_s, row_r, part_s, part_r, share_s, share_r,
):
    chunks, slots, cut = row_out.shape
    rows, width = up_ref.shape
    cap = slots // groups
    wide = 3 * PAIR
    own = grad_ref.shape[0] // seq
    g, s = lax.axis_index("group"), lax.axis_index("seq")
    order = [4, 3, 5, 2, 6, 1, 7]

    def load(b):
        return pltpu.make_async_copy(w_ref.at[pl.ds(b * width, width)], w_vm.at[b], w_s.at[b])

    load_slope = pltpu.make_async_copy(slope_ref, slope, slope_s)
    load_slope.start()
    for b in range(seq):
        load(b).start()
    barrier, greeted = greet(groups, [seq_peer(k, seq) for k in range(1, seq)], seq)
    for b in range(seq):
        d_in[b, :, wide:] = dpu_ref[b]
    d_in[s, :, :wide] = dqkv_ref[pl.ds(pl.multiple_of(s * rows, rows), rows)]
    pl.semaphore_wait(barrier, greeted)

    def hand(k):
        to = seq_peer(k, seq)
        return send(
            dqkv_ref.at[pl.ds(pl.multiple_of(to * rows, rows), rows)], d_in.at[s, :, 0:wide],
            d_s.at[k], d_r.at[k], seq=to,
        )

    mine = pl.ds(pl.multiple_of(g * cap, cap), cap)

    def give(c, k):
        to = group_peers(k, groups)
        return send(
            row_out.at[c, pl.ds(pl.multiple_of(to * cap, cap), cap)], row_in.at[c, mine],
            row_s.at[c, k], row_r.at[c, k], group=to,
        )

    def spread(c, k):
        to = seq_peer(k, seq)
        return send(part.at[c, to], part_in.at[c, s], part_s.at[c, k], part_r.at[c, k], seq=to)

    x, core = lax.div(s, 2), lax.rem(s, 2)
    sib = s + 1 - 2 * core
    chips = seq // 2

    def copy_share(c, dx):
        to = sib if dx == 0 else lax.rem(x + dx, chips) * 2 + core
        return send(share.at[c], share_in.at[c, s], share_s.at[c, dx], share_r.at[c, dx], seq=to)

    def pass_share(c, dx):
        block = lax.rem(x + chips - dx, chips) * 2 + core
        view = share_in.at[c, block]
        return send(view, view, share_s.at[c, chips + dx], share_r.at[c, chips + dx], seq=sib)

    for k in order:
        hand(k).start()
    load_slope.wait()
    for b in range(seq):
        load(b).wait()

    for c in range(chunks):
        cols = slice(c * cut, (c + 1) * cut)
        total = up_ref[:, cols].astype(F32)
        for k in [0, 7, 1, 6, 2, 5, 3, 4]:
            b = lax.rem(s + seq - k, seq)
            if c == 0 and k > 0:
                hand(k).wait_recv()
            if c == 0:
                d_in[b, :, :wide] = (d_in[b, :, :wide].astype(F32) * slope[b]).astype(BF)
            total = total + mm(d_in[b], w_vm[b, cols, :], NT)
        row_out[c] = mm(place_ref[...], total.astype(BF)).astype(BF)

        @pl.loop(1, groups)
        def _(k):
            if c > 0:
                give(c - 1, k).wait_send()
            give(c, k).start()

        row_in[c, mine] = row_out[c, mine]

    for c in range(chunks):

        @pl.loop(1, groups)
        def _(k):
            give(c, k).wait_recv()
            if c == chunks - 1:
                give(c, k).wait_send()

        sums = mm(wanted_ref[...], row_in[c], TN)
        for b in range(seq):
            part[c, b] = sums[b * own : (b + 1) * own].astype(BF)
            part_f[b] = sums[b * own : (b + 1) * own]
        for k in order:
            spread(c, k).start()
        total = part_f[s]
        for k in range(1, seq):
            spread(c, k).wait_recv()
            total = total + part_in[c, lax.rem(s + seq - k, seq)].astype(F32)
        share[c] = total
        for dx in [2, 1, 3, 0]:
            copy_share(c, dx).start()
        share_in[c, s] = total

    for c in range(chunks):
        for dx in [1, 3, 2]:
            copy_share(c, dx).wait()
            pass_share(c, dx).start()
        copy_share(c, 0).wait()
        for dx in [1, 3, 2]:
            pass_share(c, dx).wait()
        for b in range(seq):
            grad_ref[b * own : (b + 1) * own, c * cut : (c + 1) * cut] = share_in[c, b]
        for k in order:
            spread(c, k).wait_send()
    for k in order:
        hand(k).wait_send()


VM = pl.BlockSpec(memory_space=pltpu.VMEM)
SM = pl.BlockSpec(memory_space=pltpu.SMEM)
MIB = 1 << 20


def local_call(kernel, out_shape, specs, scratch=(), limit=40):
    return pl.pallas_call(
        kernel,
        out_shape=out_shape,
        in_specs=specs,
        out_specs=jax.tree.map(lambda _: VM, out_shape),
        scratch_shapes=list(scratch),
        compiler_params=pltpu.CompilerParams(vmem_limit_bytes=limit * MIB),
    )


def remote_call(kernel, ident, out_shape, specs, scratch, out_specs=None, limit=48):
    return pl.pallas_call(
        kernel,
        out_shape=out_shape,
        in_specs=specs,
        out_specs=out_specs or jax.tree.map(lambda _: VM, out_shape),
        scratch_shapes=list(scratch),
        compiler_params=pltpu.CompilerParams(
            collective_id=ident, has_side_effects=True, vmem_limit_bytes=limit * MIB
        ),
    )


ANY = pl.BlockSpec(memory_space=pl.ANY)
HBM = pl.BlockSpec(memory_space=pltpu.HBM)
CHUNKS = 2
HALVES = 2
DMA = pltpu.SemaphoreType.DMA


def sds(shape, dtype):
    return jax.ShapeDtypeStruct(shape, dtype)


def adam_update(embed_table, adam_m, adam_v, row_grad):
    new_moment = beta_first * adam_m + (1.0 - beta_first) * row_grad
    new_second = beta_second * adam_v + (1.0 - beta_second) * row_grad * row_grad
    step_size = new_moment / bias_first / (jnp.sqrt(new_second / bias_second) + adam_eps)
    new_table = embed_table.astype(F32) - learn_rate * step_size
    return (new_table, new_moment, new_second)


def body(
    embed_table,
    adam_m,
    adam_v,
    lengths,
    row_owner,
    row_index,
    proj_weight,
    out_weight,
    norm_gain,
    upstream,
):
    tok_rows = row_index.shape[0]
    groups = lax.axis_size("group")
    seq = lax.axis_size("seq")
    capacity = 2 * tok_rows // groups
    slots = groups * capacity
    tokens = tok_rows * seq
    width = embed_table.shape[1]
    table_rows = embed_table.shape[0]

    cut = width // CHUNKS

    embedded, slope, pre_u, qkv, wanted, place, w_all = remote_call(
        functools.partial(fetch_kernel, groups, seq),
        1,
        (
            sds((tok_rows, width), BF),
            sds((seq, tok_rows, 3 * PAIR), F32),
            sds((seq, tok_rows, PAIR), F32),
            sds((tokens, 3 * PAIR), BF),
            sds((slots, table_rows), BF),
            sds((slots, tok_rows), BF),
            sds((seq * width, 4 * PAIR), BF),
        ),
        [VM, HBM, HBM],
        [
            pltpu.VMEM((seq, width, 4 * PAIR), BF),
            pltpu.VMEM((table_rows, width), BF),
            pltpu.VMEM((seq, tok_rows, 3 * PAIR), BF),
            pltpu.VMEM((seq, tok_rows, 3 * PAIR), BF),
            DMA((2,)),
            DMA((seq,)),
            DMA((2, 9)),
            DMA((2, 9)),
            pltpu.VMEM((slots, PAIR), BF),
            pltpu.VMEM((slots, PAIR), BF),
            pltpu.VMEM((CHUNKS, slots, cut), BF),
            pltpu.VMEM((CHUNKS, slots, cut), BF),
            DMA((groups,)),
            DMA((groups,)),
            DMA((CHUNKS, groups)),
            DMA((CHUNKS, groups)),
            DMA((seq,)),
            DMA((seq,)),
        ],
        (VM,) * 6 + (HBM,),
        limit=57,
    )(jnp.stack([row_owner[:, 0], row_index]), embed_table, proj_weight)

    att_heads = local_call(attend_kernel, sds((tokens, PAIR), BF), [SM, VM])(lengths, qkv)
    layer_out, d_heads, d_pre_u = remote_call(
        functools.partial(middle_kernel, seq),
        2,
        (
            sds((tok_rows, width), F32),
            sds((seq, tok_rows, PAIR), BF),
            sds((seq, tok_rows, PAIR), BF),
        ),
        [VM, VM, VM, ANY, VM, VM],
        [
            pltpu.VMEM((width, width), BF),
            pltpu.VMEM((tok_rows, width), BF),
            pltpu.VMEM((seq, tok_rows, PAIR), BF),
            pltpu.VMEM((seq, tok_rows, PAIR), BF),
            pltpu.VMEM((seq, tok_rows, PAIR), BF),
            pltpu.VMEM((tok_rows, width), F32),
            DMA,
            DMA((HALVES, seq)),
            DMA((HALVES, seq)),
            DMA((HALVES, seq)),
            DMA((HALVES, seq)),
        ],
    )(att_heads, embedded, pre_u, out_weight, norm_gain.reshape(1, -1), upstream)
    d_qkv_heads = local_call(
        attend_back_kernel,
        sds((tokens, 3 * PAIR), BF),
        [SM, VM, VM],
        [pltpu.VMEM((tokens, PAIR), F32)],
    )(lengths, qkv, d_heads.reshape(tokens, PAIR))
    own = table_rows // seq
    row_grad = remote_call(
        functools.partial(back_kernel, groups, seq),
        3,
        sds((table_rows, width), F32),
        [VM, VM, VM, VM, ANY, ANY, VM],
        [
            pltpu.VMEM((seq, width, 4 * PAIR), BF),
            pltpu.VMEM((seq, tok_rows, 3 * PAIR), F32),
            DMA,
            pltpu.VMEM((seq, tok_rows, 4 * PAIR), BF),
            pltpu.VMEM((CHUNKS, slots, cut), BF),
            pltpu.VMEM((CHUNKS, slots, cut), BF),
            pltpu.VMEM((CHUNKS, seq, own, cut), BF),
            pltpu.VMEM((seq, own, cut), F32),
            pltpu.VMEM((CHUNKS, seq, own, cut), BF),
            pltpu.VMEM((CHUNKS, own, cut), F32),
            pltpu.VMEM((CHUNKS, seq, own, cut), F32),
            DMA((seq,)),
            DMA((seq,)),
            DMA((seq,)),
            DMA((CHUNKS, groups)),
            DMA((CHUNKS, groups)),
            DMA((CHUNKS, seq)),
            DMA((CHUNKS, seq)),
            DMA((CHUNKS, seq)),
            DMA((CHUNKS, seq)),
        ],
    )(d_qkv_heads, d_pre_u, place, wanted, w_all, slope, upstream)
    new_table, new_moment, new_second = adam_update(embed_table, adam_m, adam_v, row_grad)
    return (layer_out, new_table, new_moment, new_second)


def solution(mesh):
    placed = (
        P("group", None),
        P("group", None),
        P("group", None),
        P("group", None),
        P(("group", "seq"), None),
        P(("group", "seq")),
        P(None, "seq"),
        P(),
        P(),
        P(("group", "seq"), None),
    )
    return jax.shard_map(
        body,
        mesh=mesh,
        in_specs=placed,
        out_specs=(P(("group", "seq"), None), P("group", None), P("group", None), P("group", None)),
        check_vma=False,
    )
```
